512 devices in a mesh: prefix: 16 (over z_lo, x), dec: 16 (over z_hi, y), tp: 2 (over core).
Axes of the slice: x: 4, y: 8, z: 8 (z_hi: 2, z_lo: 4; z = z_hi * 4 + z_lo), core: 2. Of those that a mesh axis runs over, the one named last changes fastest.
Arguments:
- queries: bfloat16 [4096, 4096], P(('prefix', 'dec'), 'tp'), may hold values from -12 to 12
- prefix_kv: bfloat16 [16, 2, 16384, 512], P('prefix', None, 'dec', 'tp'), may hold values from -12 to 12
- suffix_kv: bfloat16 [4096, 2, 64, 512], P(('prefix', 'dec'), None, None, 'tp'), may hold values from -12 to 12
- prefix_map: int32 [4096, 1], P(('prefix', 'dec')), may hold values from 0 to 15; in each aligned block of 16 rows (0 to 15, 16 to 31, ...) at most 2 rows name the same one
- suffix_len: int32 [256, 16], P(('prefix', 'dec')), may hold values from 1 to 64, 512 in all within a row
Outputs:
- attended: bfloat16 [4096, 4096], P(('prefix', 'dec', 'tp'))
The draws below stay inside these ranges and needn't reach their ends.
Inputs may be any that keep to these rules, and one draw needn't show every extreme that they name: `prefix_map`: among the 16 requests of one device no prefix is named more than 2 times, and on some devices one prefix exactly 2 times. `suffix_len`: the 16 lengths of one device sum to 512, and the longest of them is 64.
All inputs are finite; a program needn't handle non-finite values.
Results may differ from the reference program's by a relative error of at most 0.025.
Values may be sent and summed in bfloat16 or wider, within the bound.
No kernel may reach another device: no remote copies, remote signals or barrier semaphores. Data moves between devices by JAX's collectives and lax.ppermute only.
A program may use at most 64 MiB of HBM per device.

```python
import math
import jax
import jax.numpy as jnp
import numpy as np
from jax import lax

HEAD_SIZE = 128
KEY_VALUE_HEADS = 4
QUERY_HEADS = 32
REQ_DEV = 16
PREFIX_BLOCK_LEN = 1024
SUFFIX_LIMIT = 64
PREFIX_COUNT = 16
PREFIX_LENGTH = 16384
SHARDS = 256
REQUEST_COUNT = 4096
SLOTS = 2


def shared_directions(key):
    return jnp.clip(jax.random.normal(jax.random.fold_in(key, 202), (REQUEST_COUNT, KEY_VALUE_HEADS, HEAD_SIZE), jnp.float32), -4.0, 4.0)


def draw_queries(key, part):
    directions = shared_directions(key)
    key = jax.random.fold_in(key, 1)
    key_noise, key_scale = jax.random.split(key)
    complete_shape = (REQUEST_COUNT, KEY_VALUE_HEADS, QUERY_HEADS // KEY_VALUE_HEADS, HEAD_SIZE)
    jitter = jnp.clip(jax.random.normal(key_noise, complete_shape, jnp.float32), -4.0, 4.0)
    spread = jnp.exp(jax.random.uniform(key_scale, (REQUEST_COUNT, 1, 1, 1), jnp.float32, math.log(0.5), math.log(1.5)))
    random_seed_key = 0.6 * directions[:, :, None, :] + spread * jitter
    return random_seed_key.reshape(REQUEST_COUNT, QUERY_HEADS * HEAD_SIZE).astype(jnp.bfloat16)


def draw_prefix_kv(key, part):
    key = jax.random.fold_in(key, 2)
    key_noise, key_keys, key_values = jax.random.split(key, 3)
    complete_shape = (PREFIX_COUNT, 2, PREFIX_LENGTH, KEY_VALUE_HEADS, HEAD_SIZE)
    member = jnp.arange(2).reshape(1, 2, 1, 1, 1)
    jitter = jnp.clip(jax.random.normal(key_noise, complete_shape, jnp.float32), -4.0, 4.0)
    key_spread = jnp.exp(jax.random.uniform(key_keys, (PREFIX_COUNT, 1, PREFIX_LENGTH, 1, 1), jnp.float32, math.log(0.6), math.log(1.6)))
    value_spread = jnp.exp(jax.random.uniform(key_values, (PREFIX_COUNT, 1, PREFIX_LENGTH, 1, 1), jnp.float32, math.log(0.3), math.log(3.0)))
    random_seed_key = jitter * jnp.where(member == 0, key_spread, value_spread)
    return random_seed_key.reshape(PREFIX_COUNT, 2, PREFIX_LENGTH, KEY_VALUE_HEADS * HEAD_SIZE).astype(jnp.bfloat16)


def draw_suffix_kv(key, part):
    directions = shared_directions(key)
    key = jax.random.fold_in(key, 3)
    key_noise, key_values = jax.random.split(key)
    complete_shape = (REQUEST_COUNT, 2, SUFFIX_LIMIT, KEY_VALUE_HEADS, HEAD_SIZE)
    member = jnp.arange(2).reshape(1, 2, 1, 1, 1)
    jitter = jnp.clip(jax.random.normal(key_noise, complete_shape, jnp.float32), -4.0, 4.0)
    value_spread = jnp.exp(jax.random.uniform(key_values, (REQUEST_COUNT, 1, SUFFIX_LIMIT, 1, 1), jnp.float32, math.log(0.3), math.log(3.0)))
    key_part = 0.6 * directions[:, None, None, :, :] + jitter
    random_seed_key = jnp.where(member == 0, key_part, jitter * value_spread)
    return random_seed_key.reshape(REQUEST_COUNT, 2, SUFFIX_LIMIT, KEY_VALUE_HEADS * HEAD_SIZE).astype(jnp.bfloat16)


def split_up(count, total, most, slope):
    weights = [(1 << 20) // math.isqrt(grade ** slope) + 1 for grade in range(2, count + 1)]
    spare, given = total - most - (count - 1), [1] * (count - 1)
    while spare > 0:
        free = [i for i in range(count - 1) if given[i] < most]
        whole, remaining = sum([weights[i] for i in free]), spare
        for i in free:
            more = min(most - given[i], max(1, remaining * weights[i] // whole), spare)
            given[i] = given[i] + more
            spare = spare - more
    return np.array([most] + given)


def uneven_parts(own_key, number_of, total, most, lean):
    if number_of == 2:
        one = jax.random.randint(own_key, (), max(1, total - most), min(most, total - 1) + 1)
        return jnp.stack([one, total - one])
    sizes = jnp.asarray(split_up(number_of, total, most, lean), jnp.int32)
    twos = (number_of - 1) // 2
    giver, receiver = sizes[1:1 + 2 * twos:2], sizes[2:2 + 2 * twos:2]
    slack = jnp.minimum(giver - 1, most - receiver)
    moved = jax.random.randint(jax.random.fold_in(own_key, 1), (twos,), 0, 1 << 20) % (slack + 1)
    sizes = sizes.at[1:1 + 2 * twos:2].set(giver - moved).at[2:2 + 2 * twos:2].set(receiver + moved)
    return sizes[jax.random.permutation(jax.random.fold_in(own_key, 2), number_of)]


def assign_block(own_key, own, number, rows, count, top, limit, slope):
    ranking = jax.random.permutation(own_key, count)
    heavy_load, ordinary = portions_of(count, rows * top, limit, slope, True), portions_of(count, rows * top, limit, slope, False)
    places = jnp.arange(count)

    def named(sizes, offset_by):
        used = int((sizes > 0).sum())
        fixed = max(1, used // 4)
        shifted = fixed + (places - fixed + offset_by * (used - fixed)) % max(1, count - fixed)
        return jnp.zeros((count,), jnp.int32).at[ranking[jnp.where(places < fixed, places, shifted)]].set(jnp.asarray(sizes, jnp.int32))

    sizes = jnp.where(number % 4 == 0, named(heavy_load, number // 4), named(ordinary, number - number // 4 - 1))
    mixed = jax.random.permutation(jax.random.fold_in(own, 3), count)
    source_of, taker = mixed[0:count // 2 * 2:2], mixed[1:count // 2 * 2:2]
    slack = jnp.minimum(sizes[source_of] - 1, limit - sizes[taker]) // 2
    slack = jnp.where((source_of == ranking[0]) | (taker == ranking[0]) | (sizes[taker] == 0), 0, jnp.maximum(slack, 0))
    shifted = jax.random.randint(jax.random.fold_in(own, 4), (count // 2,), 0, 1 << 20) % (slack + 1)
    sizes = sizes.at[source_of].add(-shifted).at[taker].add(shifted)
    labels = jnp.searchsorted(jnp.cumsum(sizes), jnp.arange(rows * top), side="right").astype(jnp.int32)
    grid = labels.reshape(top, rows).T
    grid = grid[jax.random.permutation(jax.random.fold_in(own, 1), rows)]
    offset_by = jax.random.randint(jax.random.fold_in(own, 2), (rows, 1), 0, top)
    return jnp.take_along_axis(grid, (jnp.arange(top)[None, :] + offset_by) % top, axis=1)


def portions_of(number_of, total, reach, lean, full):
    portions = [(1 << 20) // math.isqrt(standing ** lean) + 1 for standing in range(1, number_of + 1)]
    largest = reach if full else min(reach, max(-(-total // number_of), total * portions[0] // sum(portions)))
    least = 1 if total - largest >= number_of - 1 else 0
    given, surplus = [largest] + [least] * (number_of - 1), total - largest - least * (number_of - 1)
    while surplus > 0:
        free = [i for i in range(1, number_of) if given[i] < largest] or [i for i in range(1, number_of) if given[i] < reach]
        pool, budget = sum([portions[i] for i in free]), surplus
        for i in free:
            addition = min(reach - given[i], max(1, budget * portions[i] // pool), surplus)
            given[i] = given[i] + addition
            surplus = surplus - addition
    return np.array(given)


def setup_inputs(seed: int = 0) -> dict:
    keys = jax.random.split(jax.random.key(seed), 6)
    queries = draw_queries(jax.random.fold_in(keys[5], 71), 0)
    prefix_kv = draw_prefix_kv(jax.random.fold_in(keys[5], 71), 0)
    suffix_kv = draw_suffix_kv(jax.random.fold_in(keys[5], 71), 0)
    prefix_map_keys = jax.random.split(jax.random.fold_in(keys[3], 1), REQUEST_COUNT // REQ_DEV)
    prefix_map_turns = jax.random.permutation(jax.random.fold_in(keys[3], 3), REQUEST_COUNT // REQ_DEV)
    prefix_map = jax.vmap(lambda own, number: assign_block(jax.random.fold_in(keys[3], 2), own, number, REQ_DEV, PREFIX_COUNT, 1, SLOTS, 2))(prefix_map_keys, prefix_map_turns).reshape((REQUEST_COUNT, 1))
    suffix_len = jax.vmap(lambda own: uneven_parts(own, REQ_DEV, REQ_DEV * SUFFIX_LIMIT // 2, SUFFIX_LIMIT, 2))(jax.random.split(keys[4], SHARDS)).reshape((SHARDS, REQ_DEV)).astype(jnp.int32)
    return {"queries": queries, "prefix_kv": prefix_kv, "suffix_kv": suffix_kv, "prefix_map": prefix_map, "suffix_len": suffix_len}


def bf16_round(values):
    return lax.optimization_barrier(values.astype(jnp.bfloat16)).astype(jnp.float32)


def attend_block(request_queries, prefix_key_rows, prefix_value_rows, visible):
    scores = jnp.einsum("hgd,thd->hgt", request_queries, prefix_key_rows.astype(jnp.float32)) * (HEAD_SIZE ** -0.5)
    scores = jnp.where(visible, scores, -1.0e30)
    maxima = jnp.max(scores, axis=-1)
    weights = jnp.exp(scores - maxima[..., None]) * visible
    totals = jnp.sum(weights, axis=-1)
    rounded = bf16_round(weights)
    outputs = jnp.einsum("hgt,thd->hgd", rounded, prefix_value_rows.astype(jnp.float32))
    return maxima, totals, outputs


def reference(queries, prefix_kv, suffix_kv, prefix_map, suffix_len):
    group_list = QUERY_HEADS // KEY_VALUE_HEADS
    owners = prefix_map[:, 0].astype(jnp.int32)
    lengths = suffix_len.reshape(REQUEST_COUNT).astype(jnp.int32)
    block_list = PREFIX_LENGTH // PREFIX_BLOCK_LEN

    def one_request(request_data):
        request_queries, owner, suffix_row_count, length = request_data
        request_queries = request_queries.astype(jnp.float32).reshape(KEY_VALUE_HEADS, group_list, HEAD_SIZE)
        picked_prefix = lax.dynamic_index_in_dim(prefix_kv, owner, 0, keepdims=False)
        prefix_key_rows = picked_prefix[0].reshape(block_list, PREFIX_BLOCK_LEN, KEY_VALUE_HEADS, HEAD_SIZE)
        prefix_value_rows = picked_prefix[1].reshape(block_list, PREFIX_BLOCK_LEN, KEY_VALUE_HEADS, HEAD_SIZE)
        everywhere = jnp.ones((PREFIX_BLOCK_LEN,), dtype=jnp.bool_)
        maxima, totals, outputs = jax.vmap(attend_block, in_axes=(None, 0, 0, None))(request_queries, prefix_key_rows, prefix_value_rows, everywhere)
        summit = jnp.max(maxima, axis=0)
        factor = jnp.exp(maxima - summit)
        prefix_num = jnp.sum(bf16_round(outputs * factor[..., None]), axis=0)
        prefix_den = jnp.sum(bf16_round(totals * factor), axis=0)
        visible = jnp.arange(SUFFIX_LIMIT, dtype=jnp.int32) < length
        suffix_key_rows = suffix_row_count[0].reshape(SUFFIX_LIMIT, KEY_VALUE_HEADS, HEAD_SIZE)
        suffix_value_rows = suffix_row_count[1].reshape(SUFFIX_LIMIT, KEY_VALUE_HEADS, HEAD_SIZE)
        tail_max, tail_total, tail_out = attend_block(request_queries, suffix_key_rows, suffix_value_rows, visible)
        overall = jnp.maximum(summit, tail_max)
        prefix_weight = jnp.exp(summit - overall)
        tail_weight = jnp.exp(tail_max - overall)
        numerator = prefix_num * prefix_weight[..., None] + tail_out * tail_weight[..., None]
        denominator = prefix_den * prefix_weight + tail_total * tail_weight
        return (numerator / denominator[..., None]).astype(jnp.bfloat16).reshape(QUERY_HEADS * HEAD_SIZE)

    return lax.map(one_request, (queries, owners, suffix_kv, lengths))
```

```python
import functools
import math

import jax
import jax.numpy as jnp
from jax import lax
from jax.experimental import pallas as pl
from jax.experimental.pallas import tpu as pltpu
from jax.sharding import Mesh, PartitionSpec as P

HEAD = 128
GROUP = 8
SLOTS = 2
ROWS = SLOTS * GROUP
SCALE = HEAD ** (-0.5)
LOG2E = math.log2(math.e)
STATS = 16
Z_HALVES = 2
VMEM_LIMIT = 48 * 1024 * 1024


def iota(shape, dim):
    return lax.broadcasted_iota(jnp.int32, shape, dim)


def diagonal(size):
    return iota((size, size), 0) == iota((size, size), 1)


def to_lanes(column, eye):
    return jnp.sum(jnp.where(eye, column, 0.0), axis=0, keepdims=True)


def to_column(lanes, eye):
    return jnp.sum(jnp.where(eye, lanes, 0.0), axis=1, keepdims=True)


def slots_of(owners):
    count = owners.shape[0]
    owner_column = owners.astype(jnp.float32)
    owner_lanes = to_lanes(owner_column, diagonal(count))
    same = owner_column == owner_lanes
    row, lane = iota((count, count), 0), iota((count, count), 1)
    rank_lanes = jnp.sum(jnp.where(same & (row < lane), 1.0, 0.0), axis=0, keepdims=True)
    rank_column = jnp.sum(jnp.where(same & (lane < row), 1.0, 0.0), axis=1, keepdims=True)
    return owner_lanes * SLOTS + rank_lanes, owner_column * SLOTS + rank_column


def pieces_of(value):
    first = value.astype(jnp.bfloat16).astype(jnp.float32)
    second = (value - first).astype(jnp.bfloat16).astype(jnp.float32)
    return first, second, value - first - second


def place_kernel(owners_ref, queries_ref, out_ref):
    requests, heads = queries_ref.shape[0], queries_ref.shape[1] // HEAD
    slot_lanes, _ = slots_of(owners_ref[...])
    width = heads * requests
    spread = jnp.where(iota((requests, width), 1) % requests == iota((requests, width), 0), 1.0, 0.0)
    slot_wide = jnp.dot(
        jnp.broadcast_to(slot_lanes, (8, requests)).astype(jnp.bfloat16),
        spread.astype(jnp.bfloat16),
        preferred_element_type=jnp.float32,
    )[0:1]
    lane_code = slot_wide.astype(jnp.int32) * heads + iota((1, width), 1) // requests
    owners, halves, rows = out_ref.shape[:3]
    row = iota((owners * rows, 1), 0)
    slot = (row // rows) * SLOTS + (row // GROUP) % SLOTS
    row_code = slot * heads + (row // ROWS) % (heads // GROUP) * GROUP + row % GROUP
    pick = jnp.where(row_code == lane_code, 1.0, 0.0).astype(jnp.bfloat16)
    stacked = jnp.concatenate(
        [queries_ref[:, h * HEAD:(h + 1) * HEAD] for h in range(heads)], axis=0
    )
    placed = jnp.dot(pick, stacked, preferred_element_type=jnp.float32).astype(out_ref.dtype)
    placed = placed.reshape(owners, rows, HEAD)
    for half in range(halves):
        out_ref[:, half] = placed


def attend_kernel(count, key_ref, value_ref, *refs):
    key, value = key_ref[0, 0], value_ref[0, 0]
    wide = jnp.concatenate([value, jnp.ones_like(value)], axis=1)
    eye = diagonal(HEAD)
    blocks = HEAD // ROWS
    for query_ref, out_ref in zip(refs[:count], refs[count:]):
        size = query_ref.shape[0]
        levels = []
        for start in range(0, size, blocks):
            scores = lax.dot_general(
                query_ref[start:start + blocks].reshape(HEAD, HEAD),
                key,
                (((1,), (1,)), ((), ())),
                preferred_element_type=jnp.float32,
            )
            top = jnp.max(scores, axis=1, keepdims=True)
            weights = jnp.exp2((scores - top) * (SCALE * LOG2E))
            result = jnp.dot(weights.astype(jnp.bfloat16), wide, preferred_element_type=jnp.float32)
            total = result[:, HEAD:]
            out_ref[start:start + blocks] = (
                (result[:, :HEAD] / total).astype(out_ref.dtype).reshape(blocks, ROWS, HEAD)
            )
            levels.append(to_lanes(top * SCALE + jnp.log(total), eye))
        levels = jnp.concatenate(levels, axis=0)
        pieces = list(pieces_of(levels))
        spare = ROWS - 3 * levels.shape[0]
        if spare:
            pieces.append(jnp.zeros((spare, HEAD), jnp.float32))
        out_ref[size] = jnp.concatenate(pieces, axis=0).astype(out_ref.dtype)


def blend_kernel(sources, out_ref):
    eye = diagonal(HEAD)
    blocks = HEAD // ROWS
    kvs = (out_ref.shape[1] - STATS) // ROWS
    lane = iota((HEAD, HEAD), 1)
    for start in range(0, out_ref.shape[0], blocks):
        stats = jnp.zeros((HEAD, HEAD), jnp.float32)
        for kv in range(kvs):
            parts = []
            for refs in sources:
                offset = start
                for ref in refs:
                    size = ref.shape[0] - 1
                    if offset < size:
                        break
                    offset -= size
                groups = size // blocks
                table = ref[size, kv * ROWS:(kv + 1) * ROWS].astype(jnp.float32)
                at = offset // blocks
                level = table[at:at + 1] + table[groups + at:groups + at + 1]
                level = level + table[2 * groups + at:2 * groups + at + 1]
                mean = ref[offset:offset + blocks, kv * ROWS:(kv + 1) * ROWS].reshape(HEAD, HEAD)
                parts.append((level, mean))
            top = parts[0][0]
            for level, _ in parts[1:]:
                top = jnp.maximum(top, level)
            weights = [jnp.exp(level - top) for level, _ in parts]
            total = sum(weights)
            mixed = jnp.zeros((HEAD, HEAD), jnp.float32)
            for weight, (_, mean) in zip(weights, parts):
                mixed = mixed + mean.astype(jnp.float32) * to_column(weight / total, eye)
            out_ref[start:start + blocks, kv * ROWS:(kv + 1) * ROWS] = mixed.astype(
                out_ref.dtype
            ).reshape(blocks, ROWS, HEAD)
            column = to_column(top + jnp.log(total), eye)
            for index, piece in enumerate(pieces_of(column)):
                stats = jnp.where(lane == kv * 3 + index, piece, stats)
        out_ref[start:start + blocks, kvs * ROWS:] = stats.astype(out_ref.dtype).reshape(
            blocks, STATS, HEAD
        )


def tail_kernel(queries_ref, suffix_ref, length_ref, out_ref, max_ref, total_ref):
    requests = queries_ref.shape[0]
    limit = suffix_ref.shape[2]
    length = to_column(
        jnp.broadcast_to(length_ref[...].astype(jnp.float32), (requests, requests)), diagonal(requests)
    ).astype(jnp.int32)
    length = jnp.concatenate([length] * GROUP, axis=0)
    shape = (GROUP * requests, requests * limit)
    row, lane = iota(shape, 0), iota(shape, 1)
    shown = (lane // limit == row % requests) & (lane % limit < length)
    for kv in range(out_ref.shape[0]):
        query = jnp.concatenate(
            [
                queries_ref[:, h * HEAD:(h + 1) * HEAD]
                for h in range(kv * GROUP, (kv + 1) * GROUP)
            ],
            axis=0,
        )
        key = suffix_ref[:, 0, :, kv * HEAD:(kv + 1) * HEAD].reshape(requests * limit, HEAD)
        value = suffix_ref[:, 1, :, kv * HEAD:(kv + 1) * HEAD].reshape(requests * limit, HEAD)
        scores = lax.dot_general(
            query, key, (((1,), (1,)), ((), ())), preferred_element_type=jnp.float32
        ) * SCALE
        scores = jnp.where(shown, scores, -1e30)
        top = jnp.max(scores, axis=1, keepdims=True)
        weights = jnp.where(shown, jnp.exp(scores - top), 0.0)
        total = jnp.sum(weights, axis=1, keepdims=True)
        out_ref[kv] = jnp.dot(weights.astype(jnp.bfloat16), value, preferred_element_type=jnp.float32)
        max_ref[kv] = jnp.broadcast_to(top, max_ref.shape[1:])
        total_ref[kv] = jnp.broadcast_to(total, total_ref.shape[1:])


def merge_kernel(owners_ref, back_ref, tail_ref, max_ref, total_ref, out_ref):
    requests = owners_ref.shape[0]
    owners, halves, kvs = back_ref.shape[0], back_ref.shape[1], tail_ref.shape[0]
    _, slot = slots_of(owners_ref[...])
    slot = jnp.concatenate([slot] * GROUP, axis=0).astype(jnp.int32)
    row = iota((GROUP * requests, 1), 0)
    lane = iota((1, owners * ROWS), 1)
    pick = (slot * GROUP + row // requests) == lane
    pick = jnp.where(pick, 1.0, 0.0).astype(jnp.bfloat16)

    def picked(half, at):
        part = back_ref[:, half, at * ROWS:(at + 1) * ROWS].reshape(owners * ROWS, HEAD)
        return jnp.dot(pick, part, preferred_element_type=jnp.float32)

    stats = [picked(half, kvs) for half in range(halves)]
    for kv in range(kvs):
        levels = [
            stat[:, 3 * kv:3 * kv + 1] + stat[:, 3 * kv + 1:3 * kv + 2] + stat[:, 3 * kv + 2:3 * kv + 3]
            for stat in stats
        ]
        overall = max_ref[kv]
        for level in levels:
            overall = jnp.maximum(overall, level)
        tail_weight = jnp.exp(max_ref[kv] - overall)
        numerator = tail_ref[kv] * tail_weight
        denominator = total_ref[kv] * tail_weight
        for half, level in enumerate(levels):
            weight = jnp.exp(level - overall)
            numerator = numerator + picked(half, kv) * weight
            denominator = denominator + weight
        result = (numerator / denominator).astype(out_ref.dtype)
        for group in range(GROUP):
            head = kv * GROUP + group
            out_ref[:, head * HEAD:(head + 1) * HEAD] = result[group * requests:(group + 1) * requests]


def params():
    return pltpu.CompilerParams(vmem_limit_bytes=VMEM_LIMIT)


def place(owners, queries, owner_count):
    shape = (owner_count, Z_HALVES, SLOTS * queries.shape[1] // HEAD, HEAD)
    return pl.pallas_call(
        place_kernel,
        out_shape=jax.ShapeDtypeStruct(shape, queries.dtype),
        compiler_params=params(),
        name="place",
    )(owners, queries)


def attend(chunks, prefix_kv):
    tokens = prefix_kv.shape[2]
    kvs = prefix_kv.shape[3] // HEAD
    rows = sum(chunk.shape[0] * chunk.shape[1] for chunk in chunks)
    return pl.pallas_call(
        functools.partial(attend_kernel, len(chunks)),
        grid=(kvs,),
        in_specs=[
            pl.BlockSpec((1, 1, tokens, HEAD), lambda k: (0, 0, 0, k)),
            pl.BlockSpec((1, 1, tokens, HEAD), lambda k: (0, 1, 0, k)),
        ]
        + [pl.BlockSpec((chunk.shape[0], ROWS, HEAD), lambda k: (0, k, 0)) for chunk in chunks],
        out_specs=[
            pl.BlockSpec((chunk.shape[0] + 1, ROWS, HEAD), lambda k: (0, k, 0)) for chunk in chunks
        ],
        out_shape=[
            jax.ShapeDtypeStruct((chunk.shape[0] + 1,) + chunk.shape[1:], chunk.dtype)
            for chunk in chunks
        ],
        compiler_params=params(),
        cost_estimate=pl.CostEstimate(
            flops=8 * rows * tokens * HEAD, bytes_accessed=rows * HEAD * 4, transcendentals=rows * tokens
        ),
        name="attend",
    )(prefix_kv, prefix_kv, *chunks)


def blend(sources):
    flat = [part for parts in sources for part in parts]
    sizes = [len(parts) for parts in sources]

    def kernel(*refs):
        grouped, at = [], 0
        for size in sizes:
            grouped.append(refs[at:at + size])
            at += size
        blend_kernel(grouped, refs[-1])

    blocks = sum(part.shape[0] - 1 for part in sources[0])
    rows = flat[0].shape[1]
    return pl.pallas_call(
        kernel,
        out_shape=jax.ShapeDtypeStruct((blocks, rows + STATS, HEAD), flat[0].dtype),
        compiler_params=params(),
        name="blend",
    )(*flat)


def tail_attend(queries, suffix_kv, suffix_len):
    kvs = queries.shape[1] // (HEAD * GROUP)
    shape = jax.ShapeDtypeStruct((kvs, GROUP * queries.shape[0], HEAD), jnp.float32)
    return pl.pallas_call(
        tail_kernel,
        out_shape=[shape, shape, shape],
        compiler_params=params(),
        name="tail",
    )(queries, suffix_kv, suffix_len)


def merge(owners, back, tail, top, total, shape, dtype):
    return pl.pallas_call(
        merge_kernel,
        out_shape=jax.ShapeDtypeStruct(shape, dtype),
        compiler_params=params(),
        name="merge",
    )(owners, back, tail, top, total)


def shift(array, by):
    size = lax.axis_size("y")
    return lax.ppermute(array, "y", [(i, (i + by) % size) for i in range(size)])


def per_device(queries, prefix_kv, suffix_kv, prefix_map, suffix_len):
    owner_count = lax.axis_size("prefix")
    ring = lax.axis_size("y")
    plane = ("prefix", "zh")
    buckets = place(prefix_map, queries, owner_count)
    buckets = buckets.reshape((owner_count * Z_HALVES,) + buckets.shape[2:])
    mine = lax.all_to_all(buckets, plane, split_axis=0, concat_axis=0, tiled=True)
    half = mine.shape[0] // 2
    from_left, from_right = mine, mine
    sources = []
    steps = ring // 2
    for step in range(1, steps + 1):
        if step < steps:
            next_left, next_right = shift(from_left, 1), shift(from_right, -1)
        else:
            next_left, next_right = shift(from_left[:half], 1), shift(from_right[half:], -1)
        if step == 1:
            sources.append(attend([mine], prefix_kv))
        from_left, from_right = next_left, next_right
        to_left, to_right = attend([from_left, from_right], prefix_kv)
        if step < steps:
            sources.append([shift(to_left, -step)])
            sources.append([shift(to_right, step)])
        else:
            sources.append([shift(to_left, -step), shift(to_right, step)])
    tail, tail_max, tail_total = tail_attend(queries, suffix_kv, suffix_len)
    blended = blend(sources)
    back = lax.all_to_all(blended, plane, split_axis=0, concat_axis=0, tiled=True)
    back = back.reshape((owner_count, Z_HALVES) + back.shape[1:])
    attended = merge(prefix_map, back, tail, tail_max, tail_total, queries.shape, queries.dtype)
    return lax.all_to_all(attended, "tp", split_axis=0, concat_axis=1, tiled=True)


def solution(mesh):
    prefixes, decs, tps = mesh.devices.shape
    fine = Mesh(
        mesh.devices.reshape(prefixes, Z_HALVES, decs // Z_HALVES, tps), ("prefix", "zh", "y", "tp")
    )
    owner = ("prefix", "zh", "y")
    return jax.shard_map(
        per_device,
        mesh=fine,
        in_specs=(
            P(owner, "tp"),
            P("prefix", None, ("zh", "y"), "tp"),
            P(owner, None, None, "tp"),
            P(owner, None),
            P(owner, None),
        ),
        out_specs=P(owner + ("tp",), None),
        check_vma=False,
    )
```

```python
import functools
import math

import jax
import jax.numpy as jnp
from jax import lax
from jax.experimental import pallas as pl
from jax.experimental.pallas import tpu as pltpu
from jax.sharding import Mesh, PartitionSpec as P

HEAD = 128
GROUP = 8
SLOTS = 2
ROWS = SLOTS * GROUP
SCALE = HEAD ** (-0.5)
LOG2E = math.log2(math.e)
STATS = 16
Z_HALVES = 2
VMEM_LIMIT = 48 * 1024 * 1024


def iota(shape, dim):
    return lax.broadcasted_iota(jnp.int32, shape, dim)


def diagonal(size):
    return iota((size, size), 0) == iota((size, size), 1)


def to_lanes(column, eye):
    return jnp.sum(jnp.where(eye, column, 0.0), axis=0, keepdims=True)


def to_column(lanes, eye):
    return jnp.sum(jnp.where(eye, lanes, 0.0), axis=1, keepdims=True)


def slots_of(owners):
    count = owners.shape[0]
    owner_column = owners.astype(jnp.float32)
    owner_lanes = to_lanes(owner_column, diagonal(count))
    same = owner_column == owner_lanes
    row, lane = iota((count, count), 0), iota((count, count), 1)
    rank_lanes = jnp.sum(jnp.where(same & (row < lane), 1.0, 0.0), axis=0, keepdims=True)
    rank_column = jnp.sum(jnp.where(same & (lane < row), 1.0, 0.0), axis=1, keepdims=True)
    return owner_lanes * SLOTS + rank_lanes, owner_column * SLOTS + rank_column


def pieces_of(value):
    first = value.astype(jnp.bfloat16).astype(jnp.float32)
    second = (value - first).astype(jnp.bfloat16).astype(jnp.float32)
    return first, second, value - first - second


def place_kernel(owners_ref, queries_ref, out_ref):
    requests, heads = queries_ref.shape[0], queries_ref.shape[1] // HEAD
    slot_lanes, _ = slots_of(owners_ref[...])
    width = heads * requests
    spread = jnp.where(iota((requests, width), 1) % requests == iota((requests, width), 0), 1.0, 0.0)
    slot_wide = jnp.dot(
        jnp.broadcast_to(slot_lanes, (8, requests)).astype(jnp.bfloat16),
        spread.astype(jnp.bfloat16),
        preferred_element_type=jnp.float32,
    )[0:1]
    lane_code = slot_wide.astype(jnp.int32) * heads + iota((1, width), 1) // requests
    owners, halves, rows = out_ref.shape[:3]
    row = iota((owners * rows, 1), 0)
    slot = (row // rows) * SLOTS + (row // GROUP) % SLOTS
    row_code = slot * heads + (row // ROWS) % (heads // GROUP) * GROUP + row % GROUP
    pick = jnp.where(row_code == lane_code, 1.0, 0.0).astype(jnp.bfloat16)
    stacked = jnp.concatenate(
        [queries_ref[:, h * HEAD:(h + 1) * HEAD] for h in range(heads)], axis=0
    )
    placed = jnp.dot(pick, stacked, preferred_element_type=jnp.float32).astype(out_ref.dtype)
    placed = placed.reshape(owners, rows, HEAD)
    for half in range(halves):
        out_ref[:, half] = placed


def attend_kernel(key_ref, value_ref, far_key_ref, far_value_ref, query_ref, out_ref):
    keys = (key_ref[0, 0], far_key_ref[0, 0])
    values = (value_ref[0, 0], far_value_ref[0, 0])
    wides = [jnp.concatenate([value, jnp.ones_like(value)], axis=1) for value in values]
    eye = diagonal(HEAD)
    blocks = HEAD // ROWS
    size = query_ref.shape[0]
    levels = []
    for start in range(0, size, blocks):
        query = query_ref[start:start + blocks].reshape(HEAD, HEAD)
        scores = [
            lax.dot_general(query, key, (((1,), (1,)), ((), ())), preferred_element_type=jnp.float32)
            for key in keys
        ]
        top = jnp.max(jnp.maximum(scores[0], scores[1]), axis=1, keepdims=True)
        result = jnp.zeros((HEAD, 2 * HEAD), jnp.float32)
        for score, wide in zip(scores, wides):
            weights = jnp.exp2((score - top) * (SCALE * LOG2E))
            result = result + jnp.dot(
                weights.astype(jnp.bfloat16), wide, preferred_element_type=jnp.float32
            )
        total = result[:, HEAD:]
        out_ref[start:start + blocks] = (
            (result[:, :HEAD] / total).astype(out_ref.dtype).reshape(blocks, ROWS, HEAD)
        )
        levels.append(to_lanes(top * SCALE + jnp.log(total), eye))
    levels = jnp.concatenate(levels, axis=0)
    pieces = list(pieces_of(levels))
    spare = ROWS - 3 * levels.shape[0]
    if spare:
        pieces.append(jnp.zeros((spare, HEAD), jnp.float32))
    out_ref[size] = jnp.concatenate(pieces, axis=0).astype(out_ref.dtype)


def blend_kernel(*refs):
    sources, outs = refs[:-2], refs[-2:]
    size, rows = sources[0].shape[0] - 1, sources[0].shape[1]
    eye = diagonal(HEAD)
    blocks = HEAD // ROWS
    groups, kvs = size // blocks, rows // ROWS
    lane = iota((HEAD, HEAD), 1)
    tables = [ref[size].astype(jnp.float32) for ref in sources]
    for group in range(groups):
        out_ref = outs[group * 2 // groups]
        here = slice(group * blocks, (group + 1) * blocks)
        start = group % (groups // 2) * blocks
        there = slice(start, start + blocks)
        stats = jnp.zeros((HEAD, HEAD), jnp.float32)
        for kv in range(kvs):
            at = kv * ROWS + group
            levels = [
                table[at:at + 1]
                + table[at + groups:at + groups + 1]
                + table[at + 2 * groups:at + 2 * groups + 1]
                for table in tables
            ]
            top = functools.reduce(jnp.maximum, levels)
            weights = [jnp.exp(level - top) for level in levels]
            total = sum(weights)
            mixed = jnp.zeros((HEAD, HEAD), jnp.float32)
            for weight, ref in zip(weights, sources):
                mean = ref[here, kv * ROWS:(kv + 1) * ROWS].reshape(HEAD, HEAD).astype(jnp.float32)
                mixed = mixed + mean * to_column(weight / total, eye)
            out_ref[there, kv * ROWS:(kv + 1) * ROWS] = mixed.astype(out_ref.dtype).reshape(
                blocks, ROWS, HEAD
            )
            column = to_column(top + jnp.log(total), eye)
            for index, piece in enumerate(pieces_of(column)):
                stats = jnp.where(lane == kv * 3 + index, piece, stats)
        out_ref[there, rows:] = stats.astype(out_ref.dtype).reshape(blocks, STATS, HEAD)


def tail_kernel(queries_ref, suffix_ref, length_ref, out_ref, max_ref, total_ref):
    requests = queries_ref.shape[0]
    limit = suffix_ref.shape[2]
    length = to_column(
        jnp.broadcast_to(length_ref[...].astype(jnp.float32), (requests, requests)), diagonal(requests)
    ).astype(jnp.int32)
    length = jnp.concatenate([length] * GROUP, axis=0)
    shape = (GROUP * requests, requests * limit)
    row, lane = iota(shape, 0), iota(shape, 1)
    shown = (lane // limit == row % requests) & (lane % limit < length)
    for kv in range(out_ref.shape[0]):
        query = jnp.concatenate(
            [
                queries_ref[:, h * HEAD:(h + 1) * HEAD]
                for h in range(kv * GROUP, (kv + 1) * GROUP)
            ],
            axis=0,
        )
        key = suffix_ref[:, 0, :, kv * HEAD:(kv + 1) * HEAD].reshape(requests * limit, HEAD)
        value = suffix_ref[:, 1, :, kv * HEAD:(kv + 1) * HEAD].reshape(requests * limit, HEAD)
        scores = lax.dot_general(
            query, key, (((1,), (1,)), ((), ())), preferred_element_type=jnp.float32
        ) * SCALE
        scores = jnp.where(shown, scores, -1e30)
        top = jnp.max(scores, axis=1, keepdims=True)
        weights = jnp.where(shown, jnp.exp(scores - top), 0.0)
        total = jnp.sum(weights, axis=1, keepdims=True)
        out_ref[kv] = jnp.dot(weights.astype(jnp.bfloat16), value, preferred_element_type=jnp.float32)
        max_ref[kv] = jnp.broadcast_to(top, max_ref.shape[1:])
        total_ref[kv] = jnp.broadcast_to(total, total_ref.shape[1:])


def merge_kernel(owners_ref, back_ref, tail_ref, max_ref, total_ref, out_ref):
    requests = owners_ref.shape[0]
    owners, halves, kvs = back_ref.shape[0], back_ref.shape[1], tail_ref.shape[0]
    _, slot = slots_of(owners_ref[...])
    slot = jnp.concatenate([slot] * GROUP, axis=0).astype(jnp.int32)
    row = iota((GROUP * requests, 1), 0)
    lane = iota((1, owners * ROWS), 1)
    pick = (slot * GROUP + row // requests) == lane
    pick = jnp.where(pick, 1.0, 0.0).astype(jnp.bfloat16)

    def picked(half, at):
        part = back_ref[:, half, at * ROWS:(at + 1) * ROWS].reshape(owners * ROWS, HEAD)
        return jnp.dot(pick, part, preferred_element_type=jnp.float32)

    stats = [picked(half, kvs) for half in range(halves)]
    for kv in range(kvs):
        levels = [
            stat[:, 3 * kv:3 * kv + 1] + stat[:, 3 * kv + 1:3 * kv + 2] + stat[:, 3 * kv + 2:3 * kv + 3]
            for stat in stats
        ]
        overall = max_ref[kv]
        for level in levels:
            overall = jnp.maximum(overall, level)
        tail_weight = jnp.exp(max_ref[kv] - overall)
        numerator = tail_ref[kv] * tail_weight
        denominator = total_ref[kv] * tail_weight
        for half, level in enumerate(levels):
            weight = jnp.exp(level - overall)
            numerator = numerator + picked(half, kv) * weight
            denominator = denominator + weight
        result = (numerator / denominator).astype(out_ref.dtype)
        for group in range(GROUP):
            head = kv * GROUP + group
            out_ref[:, head * HEAD:(head + 1) * HEAD] = result[group * requests:(group + 1) * requests]


def params():
    return pltpu.CompilerParams(vmem_limit_bytes=VMEM_LIMIT)


def place(owners, queries, owner_count):
    shape = (owner_count, Z_HALVES, SLOTS * queries.shape[1] // HEAD, HEAD)
    return pl.pallas_call(
        place_kernel,
        out_shape=jax.ShapeDtypeStruct(shape, queries.dtype),
        compiler_params=params(),
        name="place",
    )(owners, queries)


def attend(query, prefix_kv, far_kv):
    tokens, kvs = prefix_kv.shape[2], prefix_kv.shape[3] // HEAD
    size, rows, width = query.shape
    key = pl.BlockSpec((1, 1, tokens, HEAD), lambda k: (0, 0, 0, k))
    value = pl.BlockSpec((1, 1, tokens, HEAD), lambda k: (0, 1, 0, k))
    return pl.pallas_call(
        attend_kernel,
        grid=(kvs,),
        in_specs=[key, value, key, value, pl.BlockSpec((size, ROWS, width), lambda k: (0, k, 0))],
        out_specs=pl.BlockSpec((size + 1, ROWS, width), lambda k: (0, k, 0)),
        out_shape=jax.ShapeDtypeStruct((size + 1, rows, width), query.dtype),
        compiler_params=params(),
        cost_estimate=pl.CostEstimate(
            flops=12 * size * rows * tokens * HEAD,
            bytes_accessed=size * rows * HEAD * 4,
            transcendentals=2 * size * rows * tokens,
        ),
        name="attend",
    )(prefix_kv, prefix_kv, far_kv, far_kv, query)


def blend(sources):
    size, rows, width = sources[0].shape
    shape = jax.ShapeDtypeStruct(((size - 1) // 2, rows + STATS, width), sources[0].dtype)
    return pl.pallas_call(
        blend_kernel,
        out_shape=[shape, shape],
        compiler_params=params(),
        name="blend",
    )(*sources)


def tail_attend(queries, suffix_kv, suffix_len):
    kvs = queries.shape[1] // (HEAD * GROUP)
    shape = jax.ShapeDtypeStruct((kvs, GROUP * queries.shape[0], HEAD), jnp.float32)
    return pl.pallas_call(
        tail_kernel,
        out_shape=[shape, shape, shape],
        compiler_params=params(),
        name="tail",
    )(queries, suffix_kv, suffix_len)


def merge(owners, back, tail, top, total, shape, dtype):
    return pl.pallas_call(
        merge_kernel,
        out_shape=jax.ShapeDtypeStruct(shape, dtype),
        compiler_params=params(),
        name="merge",
    )(owners, back, tail, top, total)


def send(array, step):
    ring, cores = lax.axis_size("y"), lax.axis_size("tp")
    pairs = []
    for at in range(ring):
        for core in range(cores):
            to = (at + (step if core == 0 else -step)) % ring
            pairs.append((at * cores + core, to * cores + core))
    return lax.ppermute(array, ("y", "tp"), pairs)


def swap(array):
    ring, cores = lax.axis_size("y"), lax.axis_size("tp")
    pairs = []
    for at in range(ring):
        for core in range(cores):
            to = (at + (1 if at % 2 == core % 2 else -1)) % ring
            pairs.append((at * cores + core, to * cores + core))
    return lax.ppermute(array, ("y", "tp"), pairs)


def per_device(queries, prefix_kv, suffix_kv, prefix_map, suffix_len):
    owner_count = lax.axis_size("prefix")
    ring = lax.axis_size("y")
    plane = ("prefix", "zh")
    odd = lax.axis_index("y") % 2
    far_kv = swap(prefix_kv)
    buckets = place(prefix_map, queries, owner_count)
    buckets = buckets.reshape((owner_count * Z_HALVES,) + buckets.shape[2:])
    mine = lax.all_to_all(buckets, plane, split_axis=0, concat_axis=0, tiled=True)
    mine, far_kv = lax.optimization_barrier((mine, far_kv))
    half = mine.shape[0] // 2
    kept = lax.dynamic_slice_in_dim(mine, odd * half, half, 0)
    given = swap(lax.dynamic_slice_in_dim(mine, (1 - odd) * half, half, 0))
    chunk = jnp.concatenate([kept, given], axis=0)
    sources = []
    for step in range(ring // 2):
        following = send(chunk, 2) if step < ring // 2 - 1 else None
        partial = attend(chunk, prefix_kv, far_kv)
        sources.append(send(partial, -2 * step) if step else partial)
        if step < ring // 2 - 1:
            chunk, _ = lax.optimization_barrier((following, partial))
    tails = tail_attend(queries, suffix_kv, suffix_len)
    kept, given = blend(sources)
    given, tails = lax.optimization_barrier((given, tails))
    given = swap(given)
    blended = jnp.where(
        odd == 0, jnp.concatenate([kept, given], axis=0), jnp.concatenate([given, kept], axis=0)
    )
    back = lax.all_to_all(blended, plane, split_axis=0, concat_axis=0, tiled=True)
    back = back.reshape((owner_count, Z_HALVES) + back.shape[1:])
    attended = merge(prefix_map, back, *tails, queries.shape, queries.dtype)
    return lax.all_to_all(attended, "tp", split_axis=0, concat_axis=1, tiled=True)


def solution(mesh):
    prefixes, decs, tps = mesh.devices.shape
    fine = Mesh(
        mesh.devices.reshape(prefixes, Z_HALVES, decs // Z_HALVES, tps), ("prefix", "zh", "y", "tp")
    )
    owner = ("prefix", "zh", "y")
    return jax.shard_map(
        per_device,
        mesh=fine,
        in_specs=(
            P(owner, "tp"),
            P("prefix", None, ("zh", "y"), "tp"),
            P(owner, None, None, "tp"),
            P(owner, None),
            P(owner, None),
        ),
        out_specs=P(owner + ("tp",), None),
        check_vma=False,
    )
```

```python
import functools
import math

import jax
import jax.numpy as jnp
from jax import lax
from jax.experimental import pallas as pl
from jax.experimental.pallas import tpu as pltpu
from jax.sharding import Mesh, PartitionSpec as P

HEAD = 128
GROUP = 8
SLOTS = 2
ROWS = SLOTS * GROUP
SCALE = HEAD ** (-0.5)
LOG2E = math.log2(math.e)
STATS = 16
Z_HALVES = 2
CLASSES = 4
VMEM_LIMIT = 48 * 1024 * 1024


def iota(shape, dim):
    return lax.broadcasted_iota(jnp.int32, shape, dim)


def diagonal(size):
    return iota((size, size), 0) == iota((size, size), 1)


def to_lanes(column, eye):
    return jnp.sum(jnp.where(eye, column, 0.0), axis=0, keepdims=True)


def to_column(lanes, eye):
    return jnp.sum(jnp.where(eye, lanes, 0.0), axis=1, keepdims=True)


def slots_of(owners):
    count = owners.shape[0]
    owner_column = owners.astype(jnp.float32)
    owner_lanes = to_lanes(owner_column, diagonal(count))
    same = owner_column == owner_lanes
    row, lane = iota((count, count), 0), iota((count, count), 1)
    rank_lanes = jnp.sum(jnp.where(same & (row < lane), 1.0, 0.0), axis=0, keepdims=True)
    rank_column = jnp.sum(jnp.where(same & (lane < row), 1.0, 0.0), axis=1, keepdims=True)
    return owner_lanes * SLOTS + rank_lanes, owner_column * SLOTS + rank_column


def pieces_of(value):
    first = value.astype(jnp.bfloat16).astype(jnp.float32)
    second = (value - first).astype(jnp.bfloat16).astype(jnp.float32)
    return first, second, value - first - second


def place_kernel(owners_ref, queries_ref, out_ref):
    requests, heads = queries_ref.shape[0], queries_ref.shape[1] // HEAD
    slot_lanes, _ = slots_of(owners_ref[...])
    width = heads * requests
    spread = jnp.where(iota((requests, width), 1) % requests == iota((requests, width), 0), 1.0, 0.0)
    slot_wide = jnp.dot(
        jnp.broadcast_to(slot_lanes, (8, requests)).astype(jnp.bfloat16),
        spread.astype(jnp.bfloat16),
        preferred_element_type=jnp.float32,
    )[0:1]
    lane_code = slot_wide.astype(jnp.int32) * heads + iota((1, width), 1) // requests
    owners, halves, rows = out_ref.shape[:3]
    row = iota((owners * rows, 1), 0)
    slot = (row // rows) * SLOTS + (row // GROUP) % SLOTS
    row_code = slot * heads + (row // ROWS) % (heads // GROUP) * GROUP + row % GROUP
    pick = jnp.where(row_code == lane_code, 1.0, 0.0).astype(jnp.bfloat16)
    stacked = jnp.concatenate(
        [queries_ref[:, h * HEAD:(h + 1) * HEAD] for h in range(heads)], axis=0
    )
    placed = jnp.dot(pick, stacked, preferred_element_type=jnp.float32).astype(out_ref.dtype)
    placed = placed.reshape(owners, rows, HEAD)
    for half in range(halves):
        out_ref[:, half] = placed


def fan_kernel(mine_ref, out_ref):
    size = mine_ref.shape[0] // 2
    for target in range(out_ref.shape[0]):
        kv, half = target // 2 % 2, target % 2
        out_ref[target] = mine_ref[half * size:(half + 1) * size, kv * ROWS:(kv + 1) * ROWS]


def attend_kernel(*refs):
    held, query_ref, out_ref = refs[:-2], refs[-2], refs[-1]
    keys = [ref[0] for ref in held]
    wides = [jnp.concatenate([ref[1], jnp.ones_like(ref[1])], axis=1) for ref in held]
    eye = diagonal(HEAD)
    blocks = HEAD // ROWS
    targets, size = out_ref.shape[0], out_ref.shape[1] - 1

    def scores_of(start):
        query = query_ref[start:start + blocks].reshape(HEAD, HEAD)
        return [
            lax.dot_general(query, key, (((1,), (1,)), ((), ())), preferred_element_type=jnp.float32)
            for key in keys
        ]

    ahead = scores_of(0)
    for target in range(targets):
        levels = []
        for start in range(0, size, blocks):
            scores = ahead
            following = target * size + start + blocks
            if following < targets * size:
                ahead = scores_of(following)
            top = jnp.max(functools.reduce(jnp.maximum, scores), axis=1, keepdims=True)
            result = jnp.zeros((HEAD, 2 * HEAD), jnp.float32)
            for score, wide in zip(scores, wides):
                weights = jnp.exp2((score - top) * (SCALE * LOG2E))
                result = result + jnp.dot(
                    weights.astype(jnp.bfloat16), wide, preferred_element_type=jnp.float32
                )
            total = result[:, HEAD:]
            out_ref[target, start:start + blocks] = (
                (result[:, :HEAD] / total).astype(out_ref.dtype).reshape(blocks, ROWS, HEAD)
            )
            levels.append(to_lanes(top * SCALE + jnp.log(total), eye))
        levels = jnp.concatenate(levels, axis=0)
        pieces = list(pieces_of(levels))
        spare = ROWS - 3 * levels.shape[0]
        if spare:
            pieces.append(jnp.zeros((spare, HEAD), jnp.float32))
        out_ref[target, size] = jnp.concatenate(pieces, axis=0).astype(out_ref.dtype)


def blend_kernel(back_ref, out_ref):
    ring, size = back_ref.shape[0], back_ref.shape[1] - 1
    kvs = (out_ref.shape[1] - STATS) // ROWS
    eye = diagonal(HEAD)
    blocks = HEAD // ROWS
    groups = size // blocks
    lane = iota((HEAD, HEAD), 1)
    table = back_ref[:, size].astype(jnp.float32)
    for half in range(2):
        for group in range(groups):
            here = slice(group * blocks, (group + 1) * blocks)
            there = slice(half * size + group * blocks, half * size + (group + 1) * blocks)
            stats = jnp.zeros((HEAD, HEAD), jnp.float32)
            for kv in range(kvs):
                members = range(2 * kv + half, ring, CLASSES)
                levels = [
                    table[source, group:group + 1]
                    + table[source, groups + group:groups + group + 1]
                    + table[source, 2 * groups + group:2 * groups + group + 1]
                    for source in members
                ]
                top = functools.reduce(jnp.maximum, levels)
                weights = [jnp.exp(level - top) for level in levels]
                total = sum(weights)
                mixed = jnp.zeros((HEAD, HEAD), jnp.float32)
                for weight, source in zip(weights, members):
                    mean = back_ref[source, here].reshape(HEAD, HEAD).astype(jnp.float32)
                    mixed = mixed + mean * to_column(weight / total, eye)
                out_ref[there, kv * ROWS:(kv + 1) * ROWS] = mixed.astype(out_ref.dtype).reshape(
                    blocks, ROWS, HEAD
                )
                column = to_column(top + jnp.log(total), eye)
                for index, piece in enumerate(pieces_of(column)):
                    stats = jnp.where(lane == kv * 3 + index, piece, stats)
            out_ref[there, kvs * ROWS:] = stats.astype(out_ref.dtype).reshape(blocks, STATS, HEAD)


def tail_kernel(queries_ref, suffix_ref, length_ref, out_ref, max_ref, total_ref):
    requests = queries_ref.shape[0]
    limit = suffix_ref.shape[2]
    length = to_column(
        jnp.broadcast_to(length_ref[...].astype(jnp.float32), (requests, requests)), diagonal(requests)
    ).astype(jnp.int32)
    length = jnp.concatenate([length] * GROUP, axis=0)
    shape = (GROUP * requests, requests * limit)
    row, lane = iota(shape, 0), iota(shape, 1)
    shown = (lane // limit == row % requests) & (lane % limit < length)
    for kv in range(out_ref.shape[0]):
        query = jnp.concatenate(
            [
                queries_ref[:, h * HEAD:(h + 1) * HEAD]
                for h in range(kv * GROUP, (kv + 1) * GROUP)
            ],
            axis=0,
        )
        key = suffix_ref[:, 0, :, kv * HEAD:(kv + 1) * HEAD].reshape(requests * limit, HEAD)
        value = suffix_ref[:, 1, :, kv * HEAD:(kv + 1) * HEAD].reshape(requests * limit, HEAD)
        scores = lax.dot_general(
            query, key, (((1,), (1,)), ((), ())), preferred_element_type=jnp.float32
        ) * SCALE
        scores = jnp.where(shown, scores, -1e30)
        top = jnp.max(scores, axis=1, keepdims=True)
        weights = jnp.where(shown, jnp.exp(scores - top), 0.0)
        total = jnp.sum(weights, axis=1, keepdims=True)
        out_ref[kv] = jnp.dot(weights.astype(jnp.bfloat16), value, preferred_element_type=jnp.float32)
        max_ref[kv] = jnp.broadcast_to(top, max_ref.shape[1:])
        total_ref[kv] = jnp.broadcast_to(total, total_ref.shape[1:])


def merge_kernel(owners_ref, back_ref, tail_ref, max_ref, total_ref, out_ref):
    requests = owners_ref.shape[0]
    owners, halves, kvs = back_ref.shape[0], back_ref.shape[1], tail_ref.shape[0]
    _, slot = slots_of(owners_ref[...])
    slot = jnp.concatenate([slot] * GROUP, axis=0).astype(jnp.int32)
    row = iota((GROUP * requests, 1), 0)
    lane = iota((1, owners * ROWS), 1)
    pick = (slot * GROUP + row // requests) == lane
    pick = jnp.where(pick, 1.0, 0.0).astype(jnp.bfloat16)

    def picked(half, at):
        part = back_ref[:, half, at * ROWS:(at + 1) * ROWS].reshape(owners * ROWS, HEAD)
        return jnp.dot(pick, part, preferred_element_type=jnp.float32)

    stats = [picked(half, kvs) for half in range(halves)]
    for kv in range(kvs):
        levels = [
            stat[:, 3 * kv:3 * kv + 1] + stat[:, 3 * kv + 1:3 * kv + 2] + stat[:, 3 * kv + 2:3 * kv + 3]
            for stat in stats
        ]
        overall = max_ref[kv]
        for level in levels:
            overall = jnp.maximum(overall, level)
        tail_weight = jnp.exp(max_ref[kv] - overall)
        numerator = tail_ref[kv] * tail_weight
        denominator = total_ref[kv] * tail_weight
        for half, level in enumerate(levels):
            weight = jnp.exp(level - overall)
            numerator = numerator + picked(half, kv) * weight
            denominator = denominator + weight
        result = (numerator / denominator).astype(out_ref.dtype)
        for group in range(GROUP):
            head = kv * GROUP + group
            out_ref[:, head * HEAD:(head + 1) * HEAD] = result[group * requests:(group + 1) * requests]


def params():
    return pltpu.CompilerParams(vmem_limit_bytes=VMEM_LIMIT)


def place(owners, queries, owner_count):
    shape = (owner_count, Z_HALVES, SLOTS * queries.shape[1] // HEAD, HEAD)
    return pl.pallas_call(
        place_kernel,
        out_shape=jax.ShapeDtypeStruct(shape, queries.dtype),
        compiler_params=params(),
        name="place",
    )(owners, queries)


def fan(mine, ring):
    shape = (ring, mine.shape[0] // 2, ROWS, HEAD)
    return pl.pallas_call(
        fan_kernel,
        out_shape=jax.ShapeDtypeStruct(shape, mine.dtype),
        compiler_params=params(),
        name="fan",
    )(mine)


def attend(query, held):
    tokens = sum(part.shape[1] for part in held)
    ring, size, rows, width = query.shape
    step = 2
    whole = pl.BlockSpec(held[0].shape, lambda i: (0, 0, 0))
    return pl.pallas_call(
        attend_kernel,
        grid=(ring // step,),
        in_specs=[whole] * len(held)
        + [pl.BlockSpec((step * size, rows, width), lambda i: (i, 0, 0))],
        out_specs=pl.BlockSpec((step, size + 1, rows, width), lambda i: (i, 0, 0, 0)),
        out_shape=jax.ShapeDtypeStruct((ring, size + 1, rows, width), query.dtype),
        compiler_params=params(),
        cost_estimate=pl.CostEstimate(
            flops=6 * ring * size * rows * tokens * HEAD,
            bytes_accessed=ring * size * rows * HEAD * 4,
            transcendentals=ring * size * rows * tokens,
        ),
        name="attend",
    )(*held, query.reshape(ring * size, rows, width))


def blend(back, kvs):
    _, size, rows, width = back.shape
    return pl.pallas_call(
        blend_kernel,
        out_shape=jax.ShapeDtypeStruct((2 * (size - 1), kvs * rows + STATS, width), back.dtype),
        compiler_params=params(),
        name="blend",
    )(back)


def tail_attend(queries, suffix_kv, suffix_len):
    kvs = queries.shape[1] // (HEAD * GROUP)
    shape = jax.ShapeDtypeStruct((kvs, GROUP * queries.shape[0], HEAD), jnp.float32)
    return pl.pallas_call(
        tail_kernel,
        out_shape=[shape, shape, shape],
        compiler_params=params(),
        name="tail",
    )(queries, suffix_kv, suffix_len)


def merge(owners, back, tail, top, total, shape, dtype):
    return pl.pallas_call(
        merge_kernel,
        out_shape=jax.ShapeDtypeStruct(shape, dtype),
        compiler_params=params(),
        name="merge",
    )(owners, back, tail, top, total)


def share(array, flip):
    ring, cores = lax.axis_size("y"), lax.axis_size("tp")
    pairs = []
    for at in range(ring):
        for core in range(cores):
            first = at - (at - 2 * core) % CLASSES
            spots = [(first + i) % ring for i in range(CLASSES)]
            to = next(spot for spot in spots if spot % CLASSES == (at % CLASSES) ^ flip)
            pairs.append((at * cores + core, to * cores + core))
    return lax.ppermute(array, ("y", "tp"), pairs)


def per_device(queries, prefix_kv, suffix_kv, prefix_map, suffix_len):
    owner_count = lax.axis_size("prefix")
    ring = lax.axis_size("y")
    plane = ("prefix", "zh")
    kvs = queries.shape[1] // (HEAD * GROUP)
    kv = lax.axis_index("y") // 2 % 2
    own = lax.dynamic_slice_in_dim(prefix_kv[0], kv * HEAD, HEAD, 2)
    other = lax.dynamic_slice_in_dim(prefix_kv[0], (1 - kv) * HEAD, HEAD, 2)
    shared = [share(own, 1), share(other, 2), share(other, 3)]
    buckets = place(prefix_map, queries, owner_count)
    buckets = buckets.reshape((owner_count * Z_HALVES,) + buckets.shape[2:])
    mine = lax.all_to_all(buckets, plane, split_axis=0, concat_axis=0, tiled=True)
    sent = fan(mine, ring)
    sent, shared = lax.optimization_barrier((sent, shared))
    query = lax.all_to_all(sent, "y", split_axis=0, concat_axis=0, tiled=True)
    partial = attend(query, [own] + shared)
    back = lax.all_to_all(partial, "y", split_axis=0, concat_axis=0, tiled=True)
    tails = tail_attend(queries, suffix_kv, suffix_len)
    blended = blend(back, kvs)
    back = lax.all_to_all(blended, plane, split_axis=0, concat_axis=0, tiled=True)
    back = back.reshape((owner_count, Z_HALVES) + back.shape[1:])
    attended = merge(prefix_map, back, *tails, queries.shape, queries.dtype)
    return lax.all_to_all(attended, "tp", split_axis=0, concat_axis=1, tiled=True)


def solution(mesh):
    prefixes, decs, tps = mesh.devices.shape
    fine = Mesh(
        mesh.devices.reshape(prefixes, Z_HALVES, decs // Z_HALVES, tps), ("prefix", "zh", "y", "tp")
    )
    owner = ("prefix", "zh", "y")
    return jax.shard_map(
        per_device,
        mesh=fine,
        in_specs=(
            P(owner, "tp"),
            P("prefix", None, ("zh", "y"), "tp"),
            P(owner, None, None, "tp"),
            P(owner, None),
            P(owner, None),
        ),
        out_specs=P(owner + ("tp",), None),
        check_vma=False,
    )
```

```python
import functools
import math

import jax
import jax.numpy as jnp
from jax import lax
from jax.experimental import pallas as pl
from jax.experimental.pallas import tpu as pltpu
from jax.sharding import Mesh, PartitionSpec as P

HEAD = 128
GROUP = 8
SLOTS = 2
ROWS = SLOTS * GROUP
SCALE = HEAD ** (-0.5)
LOG2E = math.log2(math.e)
STATS = 16
Z_HALVES = 2
CLASSES = 4
VMEM_LIMIT = 48 * 1024 * 1024


def iota(shape, dim):
    return lax.broadcasted_iota(jnp.int32, shape, dim)


def diagonal(size):
    return iota((size, size), 0) == iota((size, size), 1)


def to_lanes(column, eye):
    return jnp.sum(jnp.where(eye, column, 0.0), axis=0, keepdims=True)


def to_column(lanes, eye):
    return jnp.sum(jnp.where(eye, lanes, 0.0), axis=1, keepdims=True)


def slots_of(owners):
    count = owners.shape[0]
    owner_column = owners.astype(jnp.float32)
    owner_lanes = to_lanes(owner_column, diagonal(count))
    same = owner_column == owner_lanes
    row, lane = iota((count, count), 0), iota((count, count), 1)
    rank_lanes = jnp.sum(jnp.where(same & (row < lane), 1.0, 0.0), axis=0, keepdims=True)
    rank_column = jnp.sum(jnp.where(same & (lane < row), 1.0, 0.0), axis=1, keepdims=True)
    return owner_lanes * SLOTS + rank_lanes, owner_column * SLOTS + rank_column


def pieces_of(value):
    first = value.astype(jnp.bfloat16).astype(jnp.float32)
    second = (value - first).astype(jnp.bfloat16).astype(jnp.float32)
    return first, second, value - first - second


def place_kernel(owners_ref, queries_ref, out_ref):
    requests, heads = queries_ref.shape[0], queries_ref.shape[1] // HEAD
    slot_lanes, _ = slots_of(owners_ref[...])
    width = heads * requests
    spread = jnp.where(iota((requests, width), 1) % requests == iota((requests, width), 0), 1.0, 0.0)
    slot_wide = jnp.dot(
        jnp.broadcast_to(slot_lanes, (8, requests)).astype(jnp.bfloat16),
        spread.astype(jnp.bfloat16),
        preferred_element_type=jnp.float32,
    )[0:1]
    lane_code = slot_wide.astype(jnp.int32) * heads + iota((1, width), 1) // requests
    owners, halves, rows = out_ref.shape[:3]
    row = iota((owners * rows, 1), 0)
    slot = (row // rows) * SLOTS + (row // GROUP) % SLOTS
    row_code = slot * heads + (row // ROWS) % (heads // GROUP) * GROUP + row % GROUP
    pick = jnp.where(row_code == lane_code, 1.0, 0.0).astype(jnp.bfloat16)
    stacked = jnp.concatenate(
        [queries_ref[:, h * HEAD:(h + 1) * HEAD] for h in range(heads)], axis=0
    )
    placed = jnp.dot(pick, stacked, preferred_element_type=jnp.float32).astype(out_ref.dtype)
    placed = placed.reshape(owners, rows, HEAD)
    for half in range(halves):
        out_ref[:, half] = placed


def fan_kernel(mine_ref, out_ref):
    size = mine_ref.shape[0] // 2
    for target in range(out_ref.shape[0]):
        kv, half = target % 2, target // 2 % 2
        out_ref[target] = mine_ref[half * size:(half + 1) * size, kv * ROWS:(kv + 1) * ROWS]


def attend_kernel(*refs):
    held, query_ref, out_ref = refs[:-2], refs[-2], refs[-1]
    keys = [ref[0] for ref in held]
    wides = [jnp.concatenate([ref[1], jnp.ones_like(ref[1])], axis=1) for ref in held]
    eye = diagonal(HEAD)
    targets, size = out_ref.shape[0], out_ref.shape[1] - 1

    rows = size * ROWS

    def scores_of(target):
        query = query_ref[target * size:(target + 1) * size].reshape(rows, HEAD)
        return [
            lax.dot_general(query, key, (((1,), (1,)), ((), ())), preferred_element_type=jnp.float32)
            for key in keys
        ]

    ahead = scores_of(0)
    for target in range(targets):
        scores = ahead
        if target + 1 < targets:
            ahead = scores_of(target + 1)
        top = jnp.max(functools.reduce(jnp.maximum, scores), axis=1, keepdims=True)
        result = jnp.zeros((rows, 2 * HEAD), jnp.float32)
        for score, wide in zip(scores, wides):
            weights = jnp.exp2((score - top) * (SCALE * LOG2E))
            result = result + jnp.dot(
                weights.astype(jnp.bfloat16), wide, preferred_element_type=jnp.float32
            )
        total = result[:, HEAD:]
        out_ref[target, :size] = (
            (result[:, :HEAD] / total).astype(out_ref.dtype).reshape(size, ROWS, HEAD)
        )
        level = top * SCALE + jnp.log(total)
        levels = jnp.concatenate(
            [to_lanes(level[at:at + HEAD], eye) for at in range(0, rows, HEAD)], axis=0
        )
        pieces = list(pieces_of(levels))
        spare = ROWS - 3 * levels.shape[0]
        if spare:
            pieces.append(jnp.zeros((spare, HEAD), jnp.float32))
        out_ref[target, size] = jnp.concatenate(pieces, axis=0).astype(out_ref.dtype)


def blend_kernel(back_ref, out_ref):
    ring, size = back_ref.shape[0], back_ref.shape[1] - 1
    kvs = (out_ref.shape[1] - STATS) // ROWS
    eye = diagonal(HEAD)
    blocks = HEAD // ROWS
    groups = size // blocks
    lane = iota((HEAD, HEAD), 1)
    table = back_ref[:, size].astype(jnp.float32)
    for half in range(2):
        for group in range(groups):
            here = slice(group * blocks, (group + 1) * blocks)
            there = slice(half * size + group * blocks, half * size + (group + 1) * blocks)
            stats = jnp.zeros((HEAD, HEAD), jnp.float32)
            for kv in range(kvs):
                members = range(kv + 2 * half, ring, CLASSES)
                levels = [
                    table[source, group:group + 1]
                    + table[source, groups + group:groups + group + 1]
                    + table[source, 2 * groups + group:2 * groups + group + 1]
                    for source in members
                ]
                top = functools.reduce(jnp.maximum, levels)
                weights = [jnp.exp(level - top) for level in levels]
                total = sum(weights)
                mixed = jnp.zeros((HEAD, HEAD), jnp.float32)
                for weight, source in zip(weights, members):
                    mean = back_ref[source, here].reshape(HEAD, HEAD).astype(jnp.float32)
                    mixed = mixed + mean * to_column(weight / total, eye)
                out_ref[there, kv * ROWS:(kv + 1) * ROWS] = mixed.astype(out_ref.dtype).reshape(
                    blocks, ROWS, HEAD
                )
                column = to_column(top + jnp.log(total), eye)
                for index, piece in enumerate(pieces_of(column)):
                    stats = jnp.where(lane == kv * 3 + index, piece, stats)
            out_ref[there, kvs * ROWS:] = stats.astype(out_ref.dtype).reshape(blocks, STATS, HEAD)


def tail_kernel(queries_ref, suffix_ref, length_ref, out_ref, max_ref, total_ref):
    requests = queries_ref.shape[0]
    limit = suffix_ref.shape[2]
    length = to_column(
        jnp.broadcast_to(length_ref[...].astype(jnp.float32), (requests, requests)), diagonal(requests)
    ).astype(jnp.int32)
    length = jnp.concatenate([length] * GROUP, axis=0)
    shape = (GROUP * requests, requests * limit)
    row, lane = iota(shape, 0), iota(shape, 1)
    shown = (lane // limit == row % requests) & (lane % limit < length)
    for kv in range(out_ref.shape[0]):
        query = jnp.concatenate(
            [
                queries_ref[:, h * HEAD:(h + 1) * HEAD]
                for h in range(kv * GROUP, (kv + 1) * GROUP)
            ],
            axis=0,
        )
        key = suffix_ref[:, 0, :, kv * HEAD:(kv + 1) * HEAD].reshape(requests * limit, HEAD)
        value = suffix_ref[:, 1, :, kv * HEAD:(kv + 1) * HEAD].reshape(requests * limit, HEAD)
        scores = lax.dot_general(
            query, key, (((1,), (1,)), ((), ())), preferred_element_type=jnp.float32
        ) * SCALE
        scores = jnp.where(shown, scores, -1e30)
        top = jnp.max(scores, axis=1, keepdims=True)
        weights = jnp.where(shown, jnp.exp(scores - top), 0.0)
        total = jnp.sum(weights, axis=1, keepdims=True)
        out_ref[kv] = jnp.dot(weights.astype(jnp.bfloat16), value, preferred_element_type=jnp.float32)
        max_ref[kv] = jnp.broadcast_to(top, max_ref.shape[1:])
        total_ref[kv] = jnp.broadcast_to(total, total_ref.shape[1:])


def merge_kernel(owners_ref, back_ref, tail_ref, max_ref, total_ref, out_ref):
    requests = owners_ref.shape[0]
    owners, halves, kvs = back_ref.shape[0], back_ref.shape[1], tail_ref.shape[0]
    _, slot = slots_of(owners_ref[...])
    slot = jnp.concatenate([slot] * GROUP, axis=0).astype(jnp.int32)
    row = iota((GROUP * requests, 1), 0)
    lane = iota((1, owners * ROWS), 1)
    pick = (slot * GROUP + row // requests) == lane
    pick = jnp.where(pick, 1.0, 0.0).astype(jnp.bfloat16)

    def picked(half, at):
        part = back_ref[:, half, at * ROWS:(at + 1) * ROWS].reshape(owners * ROWS, HEAD)
        return jnp.dot(pick, part, preferred_element_type=jnp.float32)

    stats = [picked(half, kvs) for half in range(halves)]
    for kv in range(kvs):
        levels = [
            stat[:, 3 * kv:3 * kv + 1] + stat[:, 3 * kv + 1:3 * kv + 2] + stat[:, 3 * kv + 2:3 * kv + 3]
            for stat in stats
        ]
        overall = max_ref[kv]
        for level in levels:
            overall = jnp.maximum(overall, level)
        tail_weight = jnp.exp(max_ref[kv] - overall)
        numerator = tail_ref[kv] * tail_weight
        denominator = total_ref[kv] * tail_weight
        for half, level in enumerate(levels):
            weight = jnp.exp(level - overall)
            numerator = numerator + picked(half, kv) * weight
            denominator = denominator + weight
        result = (numerator / denominator).astype(out_ref.dtype)
        for group in range(GROUP):
            head = kv * GROUP + group
            out_ref[:, head * HEAD:(head + 1) * HEAD] = result[group * requests:(group + 1) * requests]


def params():
    return pltpu.CompilerParams(vmem_limit_bytes=VMEM_LIMIT)


def place(owners, queries, owner_count):
    shape = (owner_count, Z_HALVES, SLOTS * queries.shape[1] // HEAD, HEAD)
    return pl.pallas_call(
        place_kernel,
        out_shape=jax.ShapeDtypeStruct(shape, queries.dtype),
        compiler_params=params(),
        name="place",
    )(owners, queries)


def fan(mine, ring):
    shape = (ring, mine.shape[0] // 2, ROWS, HEAD)
    return pl.pallas_call(
        fan_kernel,
        out_shape=jax.ShapeDtypeStruct(shape, mine.dtype),
        compiler_params=params(),
        name="fan",
    )(mine)


def attend(query, held):
    tokens = sum(part.shape[1] for part in held)
    ring, size, rows, width = query.shape
    step = 4
    whole = pl.BlockSpec(held[0].shape, lambda i: (0, 0, 0))
    return pl.pallas_call(
        attend_kernel,
        grid=(ring // step,),
        in_specs=[whole] * len(held)
        + [pl.BlockSpec((step * size, rows, width), lambda i: (i, 0, 0))],
        out_specs=pl.BlockSpec((step, size + 1, rows, width), lambda i: (i, 0, 0, 0)),
        out_shape=jax.ShapeDtypeStruct((ring, size + 1, rows, width), query.dtype),
        compiler_params=params(),
        cost_estimate=pl.CostEstimate(
            flops=6 * ring * size * rows * tokens * HEAD,
            bytes_accessed=ring * size * rows * HEAD * 4,
            transcendentals=ring * size * rows * tokens,
        ),
        name="attend",
    )(*held, query.reshape(ring * size, rows, width))


def blend(back, kvs):
    _, size, rows, width = back.shape
    return pl.pallas_call(
        blend_kernel,
        out_shape=jax.ShapeDtypeStruct((2 * (size - 1), kvs * rows + STATS, width), back.dtype),
        compiler_params=params(),
        name="blend",
    )(back)


def tail_attend(queries, suffix_kv, suffix_len):
    kvs = queries.shape[1] // (HEAD * GROUP)
    shape = jax.ShapeDtypeStruct((kvs, GROUP * queries.shape[0], HEAD), jnp.float32)
    return pl.pallas_call(
        tail_kernel,
        out_shape=[shape, shape, shape],
        compiler_params=params(),
        name="tail",
    )(queries, suffix_kv, suffix_len)


def merge(owners, back, tail, top, total, shape, dtype):
    return pl.pallas_call(
        merge_kernel,
        out_shape=jax.ShapeDtypeStruct(shape, dtype),
        compiler_params=params(),
        name="merge",
    )(owners, back, tail, top, total)


def send(array, step):
    ring, cores = lax.axis_size("y"), lax.axis_size("tp")
    pairs = []
    for at in range(ring):
        for core in range(cores):
            to = (at + (step if core == 0 else -step)) % ring
            pairs.append((at * cores + core, to * cores + core))
    return lax.ppermute(array, ("y", "tp"), pairs)


def per_device(queries, prefix_kv, suffix_kv, prefix_map, suffix_len):
    owner_count = lax.axis_size("prefix")
    ring = lax.axis_size("y")
    plane = ("prefix", "zh")
    kvs = queries.shape[1] // (HEAD * GROUP)
    kv = lax.axis_index("y") % 2
    own = lax.dynamic_slice_in_dim(prefix_kv[0], kv * HEAD, HEAD, 2)
    other = lax.dynamic_slice_in_dim(prefix_kv[0], (1 - kv) * HEAD, HEAD, 2)
    shared = [send(other, 1), send(other, -1), send(own, -2)]
    buckets = place(prefix_map, queries, owner_count)
    buckets = buckets.reshape((owner_count * Z_HALVES,) + buckets.shape[2:])
    mine = lax.all_to_all(buckets, plane, split_axis=0, concat_axis=0, tiled=True)
    sent = fan(mine, ring)
    query = lax.all_to_all(sent, "y", split_axis=0, concat_axis=0, tiled=True)
    partial = attend(query, [own] + shared)
    partial, queries = lax.optimization_barrier((partial, queries))
    back = lax.all_to_all(partial, "y", split_axis=0, concat_axis=0, tiled=True)
    tails = tail_attend(queries, suffix_kv, suffix_len)
    blended = blend(back, kvs)
    back = lax.all_to_all(blended, plane, split_axis=0, concat_axis=0, tiled=True)
    back = back.reshape((owner_count, Z_HALVES) + back.shape[1:])
    attended = merge(prefix_map, back, *tails, queries.shape, queries.dtype)
    return lax.all_to_all(attended, "tp", split_axis=0, concat_axis=1, tiled=True)


def solution(mesh):
    prefixes, decs, tps = mesh.devices.shape
    fine = Mesh(
        mesh.devices.reshape(prefixes, Z_HALVES, decs // Z_HALVES, tps), ("prefix", "zh", "y", "tp")
    )
    owner = ("prefix", "zh", "y")
    return jax.shard_map(
        per_device,
        mesh=fine,
        in_specs=(
            P(owner, "tp"),
            P("prefix", None, ("zh", "y"), "tp"),
            P(owner, None, None, "tp"),
            P(owner, None),
            P(owner, None),
        ),
        out_specs=P(owner + ("tp",), None),
        check_vma=False,
    )
```

```python
import functools
import math

import jax
import jax.numpy as jnp
from jax import lax
from jax.experimental import pallas as pl
from jax.experimental.pallas import tpu as pltpu
from jax.sharding import Mesh, PartitionSpec as P

HEAD = 128
GROUP = 8
SLOTS = 2
ROWS = SLOTS * GROUP
SCALE = HEAD ** (-0.5)
LOG2E = math.log2(math.e)
STATS = 16
Z_HALVES = 2
CLASSES = 4
VMEM_LIMIT = 48 * 1024 * 1024


def iota(shape, dim):
    return lax.broadcasted_iota(jnp.int32, shape, dim)


def diagonal(size):
    return iota((size, size), 0) == iota((size, size), 1)


def to_lanes(column, eye):
    return jnp.sum(jnp.where(eye, column, 0.0), axis=0, keepdims=True)


def to_column(lanes, eye):
    return jnp.sum(jnp.where(eye, lanes, 0.0), axis=1, keepdims=True)


def slots_of(owners):
    count = owners.shape[0]
    owner_column = owners.astype(jnp.float32)
    owner_lanes = to_lanes(owner_column, diagonal(count))
    same = owner_column == owner_lanes
    row, lane = iota((count, count), 0), iota((count, count), 1)
    rank_lanes = jnp.sum(jnp.where(same & (row < lane), 1.0, 0.0), axis=0, keepdims=True)
    rank_column = jnp.sum(jnp.where(same & (lane < row), 1.0, 0.0), axis=1, keepdims=True)
    return owner_lanes * SLOTS + rank_lanes, owner_column * SLOTS + rank_column


def pieces_of(value):
    first = value.astype(jnp.bfloat16).astype(jnp.float32)
    second = (value - first).astype(jnp.bfloat16).astype(jnp.float32)
    return first, second, value - first - second


def place_kernel(owners_ref, queries_ref, out_ref):
    requests, heads = queries_ref.shape[0], queries_ref.shape[1] // HEAD
    slot_lanes, _ = slots_of(owners_ref[...])
    width = heads * requests
    spread = jnp.where(iota((requests, width), 1) % requests == iota((requests, width), 0), 1.0, 0.0)
    slot_wide = jnp.dot(
        jnp.broadcast_to(slot_lanes, (8, requests)).astype(jnp.bfloat16),
        spread.astype(jnp.bfloat16),
        preferred_element_type=jnp.float32,
    )[0:1]
    lane_code = slot_wide.astype(jnp.int32) * heads + iota((1, width), 1) // requests
    owners, halves, rows = out_ref.shape[:3]
    row = iota((owners * rows, 1), 0)
    slot = (row // rows) * SLOTS + (row // GROUP) % SLOTS
    row_code = slot * heads + (row // ROWS) % (heads // GROUP) * GROUP + row % GROUP
    pick = jnp.where(row_code == lane_code, 1.0, 0.0).astype(jnp.bfloat16)
    stacked = jnp.concatenate(
        [queries_ref[:, h * HEAD:(h + 1) * HEAD] for h in range(heads)], axis=0
    )
    placed = jnp.dot(pick, stacked, preferred_element_type=jnp.float32).astype(out_ref.dtype)
    placed = placed.reshape(owners, rows, HEAD)
    for half in range(halves):
        out_ref[:, half] = placed


def fan_kernel(mine_ref, out_ref):
    size = mine_ref.shape[0] // 2
    for target in range(out_ref.shape[0]):
        kv, half = target % 2, target // 2 % 2
        out_ref[target] = mine_ref[half * size:(half + 1) * size, kv * ROWS:(kv + 1) * ROWS]


def attend_kernel(*refs):
    held, query_ref, out_ref = refs[:-2], refs[-2], refs[-1]
    keys = [ref[0] for ref in held]
    wides = [jnp.concatenate([ref[1], jnp.ones_like(ref[1])], axis=1) for ref in held]
    eye = diagonal(HEAD)
    targets, size = out_ref.shape[0], out_ref.shape[1] - 1

    rows = size * ROWS

    def scores_of(target):
        query = query_ref[target * size:(target + 1) * size].reshape(rows, HEAD)
        return [
            lax.dot_general(query, key, (((1,), (1,)), ((), ())), preferred_element_type=jnp.float32)
            for key in keys
        ]

    ahead = scores_of(0)
    for target in range(targets):
        scores = ahead
        if target + 1 < targets:
            ahead = scores_of(target + 1)
        top = jnp.max(functools.reduce(jnp.maximum, scores), axis=1, keepdims=True)
        result = jnp.zeros((rows, 2 * HEAD), jnp.float32)
        for score, wide in zip(scores, wides):
            weights = jnp.exp2((score - top) * (SCALE * LOG2E))
            result = result + jnp.dot(
                weights.astype(jnp.bfloat16), wide, preferred_element_type=jnp.float32
            )
        total = result[:, HEAD:]
        out_ref[target, :size] = (
            (result[:, :HEAD] / total).astype(out_ref.dtype).reshape(size, ROWS, HEAD)
        )
        level = top * SCALE + jnp.log(total)
        levels = jnp.concatenate(
            [to_lanes(level[at:at + HEAD], eye) for at in range(0, rows, HEAD)], axis=0
        )
        pieces = list(pieces_of(levels))
        spare = ROWS - 3 * levels.shape[0]
        if spare:
            pieces.append(jnp.zeros((spare, HEAD), jnp.float32))
        out_ref[target, size] = jnp.concatenate(pieces, axis=0).astype(out_ref.dtype)


def blend_kernel(back_ref, out_ref):
    ring, size = back_ref.shape[0], back_ref.shape[1] - 1
    kvs = (out_ref.shape[1] - STATS) // ROWS
    eye = diagonal(HEAD)
    blocks = HEAD // ROWS
    groups = size // blocks
    lane = iota((HEAD, HEAD), 1)
    table = back_ref[:, size].astype(jnp.float32)
    for half in range(2):
        for group in range(groups):
            here = slice(group * blocks, (group + 1) * blocks)
            there = slice(half * size + group * blocks, half * size + (group + 1) * blocks)
            stats = jnp.zeros((HEAD, HEAD), jnp.float32)
            for kv in range(kvs):
                members = range(kv + 2 * half, ring, CLASSES)
                levels = [
                    table[source, group:group + 1]
                    + table[source, groups + group:groups + group + 1]
                    + table[source, 2 * groups + group:2 * groups + group + 1]
                    for source in members
                ]
                top = functools.reduce(jnp.maximum, levels)
                weights = [jnp.exp(level - top) for level in levels]
                total = sum(weights)
                mixed = jnp.zeros((HEAD, HEAD), jnp.float32)
                for weight, source in zip(weights, members):
                    mean = back_ref[source, here].reshape(HEAD, HEAD).astype(jnp.float32)
                    mixed = mixed + mean * to_column(weight / total, eye)
                out_ref[there, kv * ROWS:(kv + 1) * ROWS] = mixed.astype(out_ref.dtype).reshape(
                    blocks, ROWS, HEAD
                )
                column = to_column(top + jnp.log(total), eye)
                for index, piece in enumerate(pieces_of(column)):
                    stats = jnp.where(lane == kv * 3 + index, piece, stats)
            out_ref[there, kvs * ROWS:] = stats.astype(out_ref.dtype).reshape(blocks, STATS, HEAD)


def tail_kernel(queries_ref, suffix_ref, length_ref, out_ref, max_ref, total_ref):
    requests = queries_ref.shape[0]
    limit = suffix_ref.shape[2]
    length = to_column(
        jnp.broadcast_to(length_ref[...].astype(jnp.float32), (requests, requests)), diagonal(requests)
    ).astype(jnp.int32)
    length = jnp.concatenate([length] * GROUP, axis=0)
    shape = (GROUP * requests, requests * limit)
    row, lane = iota(shape, 0), iota(shape, 1)
    shown = (lane // limit == row % requests) & (lane % limit < length)
    for kv in range(out_ref.shape[0]):
        query = jnp.concatenate(
            [
                queries_ref[:, h * HEAD:(h + 1) * HEAD]
                for h in range(kv * GROUP, (kv + 1) * GROUP)
            ],
            axis=0,
        )
        key = suffix_ref[:, 0, :, kv * HEAD:(kv + 1) * HEAD].reshape(requests * limit, HEAD)
        value = suffix_ref[:, 1, :, kv * HEAD:(kv + 1) * HEAD].reshape(requests * limit, HEAD)
        scores = lax.dot_general(
            query, key, (((1,), (1,)), ((), ())), preferred_element_type=jnp.float32
        ) * SCALE
        scores = jnp.where(shown, scores, -1e30)
        top = jnp.max(scores, axis=1, keepdims=True)
        weights = jnp.where(shown, jnp.exp(scores - top), 0.0)
        total = jnp.sum(weights, axis=1, keepdims=True)
        out_ref[kv] = jnp.dot(weights.astype(jnp.bfloat16), value, preferred_element_type=jnp.float32)
        max_ref[kv] = jnp.broadcast_to(top, max_ref.shape[1:])
        total_ref[kv] = jnp.broadcast_to(total, total_ref.shape[1:])


def merge_kernel(owners_ref, back_ref, tail_ref, max_ref, total_ref, out_ref):
    requests = owners_ref.shape[0]
    owners, halves, kvs = back_ref.shape[0], back_ref.shape[1], tail_ref.shape[0]
    _, slot = slots_of(owners_ref[...])
    slot = jnp.concatenate([slot] * GROUP, axis=0).astype(jnp.int32)
    row = iota((GROUP * requests, 1), 0)
    lane = iota((1, owners * ROWS), 1)
    pick = (slot * GROUP + row // requests) == lane
    pick = jnp.where(pick, 1.0, 0.0).astype(jnp.bfloat16)

    def picked(half, at):
        part = back_ref[:, half, at * ROWS:(at + 1) * ROWS].reshape(owners * ROWS, HEAD)
        return jnp.dot(pick, part, preferred_element_type=jnp.float32)

    stats = [picked(half, kvs) for half in range(halves)]
    for kv in range(kvs):
        levels = [
            stat[:, 3 * kv:3 * kv + 1] + stat[:, 3 * kv + 1:3 * kv + 2] + stat[:, 3 * kv + 2:3 * kv + 3]
            for stat in stats
        ]
        overall = max_ref[kv]
        for level in levels:
            overall = jnp.maximum(overall, level)
        tail_weight = jnp.exp(max_ref[kv] - overall)
        numerator = tail_ref[kv] * tail_weight
        denominator = total_ref[kv] * tail_weight
        for half, level in enumerate(levels):
            weight = jnp.exp(level - overall)
            numerator = numerator + picked(half, kv) * weight
            denominator = denominator + weight
        result = (numerator / denominator).astype(out_ref.dtype)
        for group in range(GROUP):
            head = kv * GROUP + group
            out_ref[:, head * HEAD:(head + 1) * HEAD] = result[group * requests:(group + 1) * requests]


def params():
    return pltpu.CompilerParams(vmem_limit_bytes=VMEM_LIMIT)


def place(owners, queries, owner_count):
    shape = (owner_count, Z_HALVES, SLOTS * queries.shape[1] // HEAD, HEAD)
    return pl.pallas_call(
        place_kernel,
        out_shape=jax.ShapeDtypeStruct(shape, queries.dtype),
        compiler_params=params(),
        name="place",
    )(owners, queries)


def fan(mine, ring):
    shape = (ring, mine.shape[0] // 2, ROWS, HEAD)
    return pl.pallas_call(
        fan_kernel,
        out_shape=jax.ShapeDtypeStruct(shape, mine.dtype),
        compiler_params=params(),
        name="fan",
    )(mine)


def attend(query, held):
    tokens = sum(part.shape[1] for part in held)
    ring, size, rows, width = query.shape
    step = 4
    whole = pl.BlockSpec(memory_space=pltpu.VMEM)
    return pl.pallas_call(
        attend_kernel,
        grid=(ring // step,),
        in_specs=[whole] * len(held)
        + [pl.BlockSpec((step * size, rows, width), lambda i: (i, 0, 0))],
        out_specs=pl.BlockSpec((step, size + 1, rows, width), lambda i: (i, 0, 0, 0)),
        out_shape=jax.ShapeDtypeStruct((ring, size + 1, rows, width), query.dtype),
        compiler_params=params(),
        cost_estimate=pl.CostEstimate(
            flops=6 * ring * size * rows * tokens * HEAD,
            bytes_accessed=ring * size * rows * HEAD * 4,
            transcendentals=ring * size * rows * tokens,
        ),
        name="attend",
    )(*held, query.reshape(ring * size, rows, width))


def blend(back, kvs):
    _, size, rows, width = back.shape
    return pl.pallas_call(
        blend_kernel,
        out_shape=jax.ShapeDtypeStruct((2 * (size - 1), kvs * rows + STATS, width), back.dtype),
        compiler_params=params(),
        name="blend",
    )(back)


def tail_attend(queries, suffix_kv, suffix_len):
    kvs = queries.shape[1] // (HEAD * GROUP)
    shape = jax.ShapeDtypeStruct((kvs, GROUP * queries.shape[0], HEAD), jnp.float32)
    return pl.pallas_call(
        tail_kernel,
        out_shape=[shape, shape, shape],
        compiler_params=params(),
        name="tail",
    )(queries, suffix_kv, suffix_len)


def merge(owners, back, tail, top, total, shape, dtype):
    return pl.pallas_call(
        merge_kernel,
        out_shape=jax.ShapeDtypeStruct(shape, dtype),
        compiler_params=params(),
        name="merge",
    )(owners, back, tail, top, total)


def send(array, step):
    ring, cores = lax.axis_size("y"), lax.axis_size("tp")
    pairs = []
    for at in range(ring):
        for core in range(cores):
            to = (at + (step if core == 0 else -step)) % ring
            pairs.append((at * cores + core, to * cores + core))
    return lax.ppermute(array, ("y", "tp"), pairs)


def per_device(queries, prefix_kv, suffix_kv, prefix_map, suffix_len):
    owner_count = lax.axis_size("prefix")
    ring = lax.axis_size("y")
    plane = ("prefix", "zh")
    kvs = queries.shape[1] // (HEAD * GROUP)
    kv = lax.axis_index("y") % 2
    own = lax.dynamic_slice_in_dim(prefix_kv[0], kv * HEAD, HEAD, 2)
    other = lax.dynamic_slice_in_dim(prefix_kv[0], (1 - kv) * HEAD, HEAD, 2)
    shared = [send(other, 1), send(other, -1), send(own, -2)]
    buckets = place(prefix_map, queries, owner_count)
    buckets = buckets.reshape((owner_count * Z_HALVES,) + buckets.shape[2:])
    mine = lax.all_to_all(buckets, plane, split_axis=0, concat_axis=0, tiled=True)
    sent = fan(mine, ring)
    sent, shared = lax.optimization_barrier((sent, shared))
    query = lax.all_to_all(sent, "y", split_axis=0, concat_axis=0, tiled=True)
    partial = attend(query, [own] + shared)
    partial, queries = lax.optimization_barrier((partial, queries))
    back = lax.all_to_all(partial, "y", split_axis=0, concat_axis=0, tiled=True)
    tails = tail_attend(queries, suffix_kv, suffix_len)
    blended = blend(back, kvs)
    back = lax.all_to_all(blended, plane, split_axis=0, concat_axis=0, tiled=True)
    back = back.reshape((owner_count, Z_HALVES) + back.shape[1:])
    attended = merge(prefix_map, back, *tails, queries.shape, queries.dtype)
    return lax.all_to_all(attended, "tp", split_axis=0, concat_axis=1, tiled=True)


def solution(mesh):
    prefixes, decs, tps = mesh.devices.shape
    fine = Mesh(
        mesh.devices.reshape(prefixes, Z_HALVES, decs // Z_HALVES, tps), ("prefix", "zh", "y", "tp")
    )
    owner = ("prefix", "zh", "y")
    return jax.shard_map(
        per_device,
        mesh=fine,
        in_specs=(
            P(owner, "tp"),
            P("prefix", None, ("zh", "y"), "tp"),
            P(owner, None, None, "tp"),
            P(owner, None),
            P(owner, None),
        ),
        out_specs=P(owner + ("tp",), None),
        check_vma=False,
    )
```

```python
import functools
import math

import jax
import jax.numpy as jnp
from jax import lax
from jax.experimental import pallas as pl
from jax.experimental.pallas import tpu as pltpu
from jax.sharding import Mesh, PartitionSpec as P

HEAD = 128
GROUP = 8
SLOTS = 2
ROWS = SLOTS * GROUP
SCALE = HEAD ** (-0.5)
LOG2E = math.log2(math.e)
STATS = 16
Z_HALVES = 2
CLASSES = 4
VMEM_LIMIT = 48 * 1024 * 1024


def iota(shape, dim):
    return lax.broadcasted_iota(jnp.int32, shape, dim)


def diagonal(size):
    return iota((size, size), 0) == iota((size, size), 1)


def to_lanes(column, eye):
    return jnp.sum(jnp.where(eye, column, 0.0), axis=0, keepdims=True)


def to_column(lanes, eye):
    return jnp.sum(jnp.where(eye, lanes, 0.0), axis=1, keepdims=True)


def slots_of(owners):
    count = owners.shape[0]
    owner_column = owners.astype(jnp.float32)
    owner_lanes = to_lanes(owner_column, diagonal(count))
    same = owner_column == owner_lanes
    row, lane = iota((count, count), 0), iota((count, count), 1)
    rank_lanes = jnp.sum(jnp.where(same & (row < lane), 1.0, 0.0), axis=0, keepdims=True)
    rank_column = jnp.sum(jnp.where(same & (lane < row), 1.0, 0.0), axis=1, keepdims=True)
    return owner_lanes * SLOTS + rank_lanes, owner_column * SLOTS + rank_column


def pieces_of(value):
    first = value.astype(jnp.bfloat16).astype(jnp.float32)
    second = (value - first).astype(jnp.bfloat16).astype(jnp.float32)
    return first, second, value - first - second


def place_kernel(owners_ref, queries_ref, out_ref):
    requests, heads = queries_ref.shape[0], queries_ref.shape[1] // HEAD
    slot_lanes, _ = slots_of(owners_ref[...])
    width = heads * requests
    spread = jnp.where(iota((requests, width), 1) % requests == iota((requests, width), 0), 1.0, 0.0)
    slot_wide = jnp.dot(
        jnp.broadcast_to(slot_lanes, (8, requests)).astype(jnp.bfloat16),
        spread.astype(jnp.bfloat16),
        preferred_element_type=jnp.float32,
    )[0:1]
    lane_code = slot_wide.astype(jnp.int32) * heads + iota((1, width), 1) // requests
    owners, halves, rows = out_ref.shape[:3]
    row = iota((owners * rows, 1), 0)
    slot = (row // rows) * SLOTS + (row // GROUP) % SLOTS
    row_code = slot * heads + (row // ROWS) % (heads // GROUP) * GROUP + row % GROUP
    pick = jnp.where(row_code == lane_code, 1.0, 0.0).astype(jnp.bfloat16)
    stacked = jnp.concatenate(
        [queries_ref[:, h * HEAD:(h + 1) * HEAD] for h in range(heads)], axis=0
    )
    placed = jnp.dot(pick, stacked, preferred_element_type=jnp.float32).astype(out_ref.dtype)
    placed = placed.reshape(owners, rows, HEAD)
    for half in range(halves):
        out_ref[:, half] = placed


def fan_kernel(mine_ref, out_ref):
    size = mine_ref.shape[0] // 2
    for target in range(out_ref.shape[0]):
        kv, half = target % 2, target // 2 % 2
        out_ref[target] = mine_ref[half * size:(half + 1) * size, kv * ROWS:(kv + 1) * ROWS]


def attend_kernel(count, *refs):
    held, query_ref, out_ref = refs[:count], refs[count], refs[count + 1]
    first_ref, second_ref, wide_ref = refs[count + 2:]
    eye = diagonal(HEAD)
    targets, size = out_ref.shape[0], out_ref.shape[1] - 1
    rows = size * ROWS
    for index, ref in enumerate(held):
        wide_ref[index] = jnp.concatenate([ref[1], jnp.ones_like(ref[1])], axis=1)

    def score(slot_ref, target):
        query = query_ref[pl.ds(target * size, size)].reshape(rows, HEAD)
        for index, ref in enumerate(held):
            slot_ref[index] = lax.dot_general(
                query, ref[0], (((1,), (1,)), ((), ())), preferred_element_type=jnp.float32
            )

    def finish(slot_ref, target):
        scores = [slot_ref[index] for index in range(count)]
        top = jnp.max(functools.reduce(jnp.maximum, scores), axis=1, keepdims=True)
        result = jnp.zeros((rows, 2 * HEAD), jnp.float32)
        for index in range(count):
            weights = jnp.exp2((slot_ref[index] - top) * (SCALE * LOG2E))
            result = result + jnp.dot(
                weights.astype(jnp.bfloat16), wide_ref[index], preferred_element_type=jnp.float32
            )
        total = result[:, HEAD:]
        out_ref[target, :size] = (
            (result[:, :HEAD] / total).astype(out_ref.dtype).reshape(size, ROWS, HEAD)
        )
        level = top * SCALE + jnp.log(total)
        levels = jnp.concatenate(
            [to_lanes(level[at:at + HEAD], eye) for at in range(0, rows, HEAD)], axis=0
        )
        pieces = list(pieces_of(levels))
        spare = ROWS - 3 * levels.shape[0]
        if spare:
            pieces.append(jnp.zeros((spare, HEAD), jnp.float32))
        out_ref[target, size] = jnp.concatenate(pieces, axis=0).astype(out_ref.dtype)

    score(first_ref, 0)

    def pair(index, carry):
        target = 2 * index
        score(second_ref, target + 1)
        finish(first_ref, target)
        score(first_ref, jnp.minimum(target + 2, targets - 1))
        finish(second_ref, target + 1)
        return carry

    lax.fori_loop(0, targets // 2, pair, 0)


def blend_kernel(back_ref, out_ref):
    ring, size = back_ref.shape[0], back_ref.shape[1] - 1
    kvs = (out_ref.shape[1] - STATS) // ROWS
    blocks = HEAD // ROWS
    groups = size // blocks
    lane = iota((HEAD, HEAD), 1)
    table = back_ref[:, size].astype(jnp.float32)
    lanes, places = [], []
    for half in range(2):
        for group in range(groups):
            for kv in range(kvs):
                members = range(kv + 2 * half, ring, CLASSES)
                levels = [
                    table[source, group:group + 1]
                    + table[source, groups + group:groups + group + 1]
                    + table[source, 2 * groups + group:2 * groups + group + 1]
                    for source in members
                ]
                top = functools.reduce(jnp.maximum, levels)
                weights = [jnp.exp(level - top) for level in levels]
                total = sum(weights)
                places.append((half, group, kv, members, len(lanes)))
                lanes += [weight / total for weight in weights] + [top + jnp.log(total)]
    lanes += [jnp.zeros((1, HEAD), jnp.float32)] * (-len(lanes) % 8)
    columns = jnp.transpose(jnp.concatenate(lanes, axis=0))
    stats = None
    for half, group, kv, members, at in places:
        here = slice(group * blocks, (group + 1) * blocks)
        there = slice(half * size + group * blocks, half * size + (group + 1) * blocks)
        mixed = jnp.zeros((HEAD, HEAD), jnp.float32)
        for index, source in enumerate(members):
            mean = back_ref[source, here].reshape(HEAD, HEAD).astype(jnp.float32)
            mixed = mixed + mean * columns[:, at + index:at + index + 1]
        out_ref[there, kv * ROWS:(kv + 1) * ROWS] = mixed.astype(out_ref.dtype).reshape(
            blocks, ROWS, HEAD
        )
        stats = jnp.zeros((HEAD, HEAD), jnp.float32) if kv == 0 else stats
        level = columns[:, at + len(members):at + len(members) + 1]
        for index, piece in enumerate(pieces_of(level)):
            stats = jnp.where(lane == kv * 3 + index, piece, stats)
        if kv == kvs - 1:
            out_ref[there, kvs * ROWS:] = stats.astype(out_ref.dtype).reshape(blocks, STATS, HEAD)


def tail_kernel(queries_ref, suffix_ref, length_ref, out_ref, max_ref, total_ref):
    requests = queries_ref.shape[0]
    limit = suffix_ref.shape[2]
    length = to_column(
        jnp.broadcast_to(length_ref[...].astype(jnp.float32), (requests, requests)), diagonal(requests)
    ).astype(jnp.int32)
    length = jnp.concatenate([length] * GROUP, axis=0)
    shape = (GROUP * requests, requests * limit)
    row, lane = iota(shape, 0), iota(shape, 1)
    shown = (lane // limit == row % requests) & (lane % limit < length)
    for kv in range(out_ref.shape[0]):
        query = jnp.concatenate(
            [
                queries_ref[:, h * HEAD:(h + 1) * HEAD]
                for h in range(kv * GROUP, (kv + 1) * GROUP)
            ],
            axis=0,
        )
        key = suffix_ref[:, 0, :, kv * HEAD:(kv + 1) * HEAD].reshape(requests * limit, HEAD)
        value = suffix_ref[:, 1, :, kv * HEAD:(kv + 1) * HEAD].reshape(requests * limit, HEAD)
        scores = lax.dot_general(
            query, key, (((1,), (1,)), ((), ())), preferred_element_type=jnp.float32
        ) * SCALE
        scores = jnp.where(shown, scores, -1e30)
        top = jnp.max(scores, axis=1, keepdims=True)
        weights = jnp.where(shown, jnp.exp(scores - top), 0.0)
        total = jnp.sum(weights, axis=1, keepdims=True)
        out_ref[kv] = jnp.dot(weights.astype(jnp.bfloat16), value, preferred_element_type=jnp.float32)
        max_ref[kv] = jnp.broadcast_to(top, max_ref.shape[1:])
        total_ref[kv] = jnp.broadcast_to(total, total_ref.shape[1:])


def merge_kernel(owners_ref, back_ref, tail_ref, max_ref, total_ref, out_ref):
    requests = owners_ref.shape[0]
    owners, halves, kvs = back_ref.shape[0], back_ref.shape[1], tail_ref.shape[0]
    _, slot = slots_of(owners_ref[...])
    slot = jnp.concatenate([slot] * GROUP, axis=0).astype(jnp.int32)
    row = iota((GROUP * requests, 1), 0)
    lane = iota((1, owners * ROWS), 1)
    pick = (slot * GROUP + row // requests) == lane
    pick = jnp.where(pick, 1.0, 0.0).astype(jnp.bfloat16)

    def picked(half, at):
        part = back_ref[:, half, at * ROWS:(at + 1) * ROWS].reshape(owners * ROWS, HEAD)
        return jnp.dot(pick, part, preferred_element_type=jnp.float32)

    stats = [picked(half, kvs) for half in range(halves)]
    for kv in range(kvs):
        levels = [
            stat[:, 3 * kv:3 * kv + 1] + stat[:, 3 * kv + 1:3 * kv + 2] + stat[:, 3 * kv + 2:3 * kv + 3]
            for stat in stats
        ]
        overall = max_ref[kv]
        for level in levels:
            overall = jnp.maximum(overall, level)
        tail_weight = jnp.exp(max_ref[kv] - overall)
        numerator = tail_ref[kv] * tail_weight
        denominator = total_ref[kv] * tail_weight
        for half, level in enumerate(levels):
            weight = jnp.exp(level - overall)
            numerator = numerator + picked(half, kv) * weight
            denominator = denominator + weight
        result = (numerator / denominator).astype(out_ref.dtype)
        for group in range(GROUP):
            head = kv * GROUP + group
            out_ref[:, head * HEAD:(head + 1) * HEAD] = result[group * requests:(group + 1) * requests]


def params():
    return pltpu.CompilerParams(vmem_limit_bytes=VMEM_LIMIT)


def place(owners, queries, owner_count):
    shape = (owner_count, Z_HALVES, SLOTS * queries.shape[1] // HEAD, HEAD)
    return pl.pallas_call(
        place_kernel,
        out_shape=jax.ShapeDtypeStruct(shape, queries.dtype),
        compiler_params=params(),
        name="place",
    )(owners, queries)


def fan(mine, ring):
    shape = (ring, mine.shape[0] // 2, ROWS, HEAD)
    return pl.pallas_call(
        fan_kernel,
        out_shape=jax.ShapeDtypeStruct(shape, mine.dtype),
        compiler_params=params(),
        name="fan",
    )(mine)


def attend(query, held):
    count, tokens = len(held), held[0].shape[1]
    ring, size, rows, width = query.shape
    slot = pltpu.VMEM((count, size * rows, tokens), jnp.float32)
    total = ring * size * rows
    return pl.pallas_call(
        functools.partial(attend_kernel, count),
        in_specs=[pl.BlockSpec(memory_space=pltpu.VMEM)] * (count + 1),
        out_specs=pl.BlockSpec(memory_space=pltpu.VMEM),
        out_shape=jax.ShapeDtypeStruct((ring, size + 1, rows, width), query.dtype),
        scratch_shapes=[slot, slot, pltpu.VMEM((count, tokens, 2 * HEAD), query.dtype)],
        compiler_params=params(),
        cost_estimate=pl.CostEstimate(
            flops=6 * total * count * tokens * HEAD,
            bytes_accessed=total * HEAD * 4,
            transcendentals=total * count * tokens,
        ),
        name="attend",
    )(*held, query.reshape(ring * size, rows, width))


def blend(back, kvs):
    _, size, rows, width = back.shape
    return pl.pallas_call(
        blend_kernel,
        out_shape=jax.ShapeDtypeStruct((2 * (size - 1), kvs * rows + STATS, width), back.dtype),
        compiler_params=params(),
        name="blend",
    )(back)


def tail_attend(queries, suffix_kv, suffix_len):
    kvs = queries.shape[1] // (HEAD * GROUP)
    shape = jax.ShapeDtypeStruct((kvs, GROUP * queries.shape[0], HEAD), jnp.float32)
    return pl.pallas_call(
        tail_kernel,
        out_shape=[shape, shape, shape],
        compiler_params=params(),
        name="tail",
    )(queries, suffix_kv, suffix_len)


def merge(owners, back, tail, top, total, shape, dtype):
    return pl.pallas_call(
        merge_kernel,
        out_shape=jax.ShapeDtypeStruct(shape, dtype),
        compiler_params=params(),
        name="merge",
    )(owners, back, tail, top, total)


def send(array, step):
    ring, cores = lax.axis_size("y"), lax.axis_size("tp")
    pairs = []
    for at in range(ring):
        for core in range(cores):
            to = (at + (step if core == 0 else -step)) % ring
            pairs.append((at * cores + core, to * cores + core))
    return lax.ppermute(array, ("y", "tp"), pairs)


def per_device(queries, prefix_kv, suffix_kv, prefix_map, suffix_len):
    owner_count = lax.axis_size("prefix")
    ring = lax.axis_size("y")
    plane = ("prefix", "zh")
    kvs = queries.shape[1] // (HEAD * GROUP)
    kv = lax.axis_index("y") % 2
    own = lax.dynamic_slice_in_dim(prefix_kv[0], kv * HEAD, HEAD, 2)
    other = lax.dynamic_slice_in_dim(prefix_kv[0], (1 - kv) * HEAD, HEAD, 2)
    shared = [send(own, -2), send(other, 1), send(other, -1)]
    buckets = place(prefix_map, queries, owner_count)
    buckets = buckets.reshape((owner_count * Z_HALVES,) + buckets.shape[2:])
    mine = lax.all_to_all(buckets, plane, split_axis=0, concat_axis=0, tiled=True)
    sent = fan(mine, ring)
    sent, shared = lax.optimization_barrier((sent, shared))
    query = lax.all_to_all(sent, "y", split_axis=0, concat_axis=0, tiled=True)
    partial = attend(query, [own] + shared)
    partial, queries = lax.optimization_barrier((partial, queries))
    back = lax.all_to_all(partial, "y", split_axis=0, concat_axis=0, tiled=True)
    tails = tail_attend(queries, suffix_kv, suffix_len)
    blended = blend(back, kvs)
    back = lax.all_to_all(blended, plane, split_axis=0, concat_axis=0, tiled=True)
    back = back.reshape((owner_count, Z_HALVES) + back.shape[1:])
    attended = merge(prefix_map, back, *tails, queries.shape, queries.dtype)
    return lax.all_to_all(attended, "tp", split_axis=0, concat_axis=1, tiled=True)


def solution(mesh):
    prefixes, decs, tps = mesh.devices.shape
    fine = Mesh(
        mesh.devices.reshape(prefixes, Z_HALVES, decs // Z_HALVES, tps), ("prefix", "zh", "y", "tp")
    )
    owner = ("prefix", "zh", "y")
    return jax.shard_map(
        per_device,
        mesh=fine,
        in_specs=(
            P(owner, "tp"),
            P("prefix", None, ("zh", "y"), "tp"),
            P(owner, None, None, "tp"),
            P(owner, None),
            P(owner, None),
        ),
        out_specs=P(owner + ("tp",), None),
        check_vma=False,
    )
```

```python
import functools
import math

import jax
import jax.numpy as jnp
from jax import lax
from jax.experimental import pallas as pl
from jax.experimental.pallas import tpu as pltpu
from jax.sharding import Mesh, PartitionSpec as P

HEAD = 128
GROUP = 8
SLOTS = 2
ROWS = SLOTS * GROUP
SCALE = HEAD ** (-0.5)
LOG2E = math.log2(math.e)
STATS = 16
Z_HALVES = 2
CLASSES = 4
VMEM_LIMIT = 48 * 1024 * 1024


def iota(shape, dim):
    return lax.broadcasted_iota(jnp.int32, shape, dim)


def diagonal(size):
    return iota((size, size), 0) == iota((size, size), 1)


def to_lanes(column, eye):
    return jnp.sum(jnp.where(eye, column, 0.0), axis=0, keepdims=True)


def to_column(lanes, eye):
    return jnp.sum(jnp.where(eye, lanes, 0.0), axis=1, keepdims=True)


def slots_of(owners):
    count = owners.shape[0]
    owner_column = owners.astype(jnp.float32)
    owner_lanes = to_lanes(owner_column, diagonal(count))
    same = owner_column == owner_lanes
    row, lane = iota((count, count), 0), iota((count, count), 1)
    rank_lanes = jnp.sum(jnp.where(same & (row < lane), 1.0, 0.0), axis=0, keepdims=True)
    rank_column = jnp.sum(jnp.where(same & (lane < row), 1.0, 0.0), axis=1, keepdims=True)
    return owner_lanes * SLOTS + rank_lanes, owner_column * SLOTS + rank_column


def pieces_of(value):
    first = value.astype(jnp.bfloat16).astype(jnp.float32)
    second = (value - first).astype(jnp.bfloat16).astype(jnp.float32)
    return first, second, value - first - second


def place_kernel(owners_ref, queries_ref, out_ref):
    requests, heads = queries_ref.shape[0], queries_ref.shape[1] // HEAD
    slot_lanes, _ = slots_of(owners_ref[...])
    width = heads * requests
    spread = jnp.where(iota((requests, width), 1) % requests == iota((requests, width), 0), 1.0, 0.0)
    slot_wide = jnp.dot(
        jnp.broadcast_to(slot_lanes, (8, requests)).astype(jnp.bfloat16),
        spread.astype(jnp.bfloat16),
        preferred_element_type=jnp.float32,
    )[0:1]
    lane_code = slot_wide.astype(jnp.int32) * heads + iota((1, width), 1) // requests
    owners, halves, rows = out_ref.shape[:3]
    row = iota((owners * rows, 1), 0)
    slot = (row // rows) * SLOTS + (row // GROUP) % SLOTS
    row_code = slot * heads + (row // ROWS) % (heads // GROUP) * GROUP + row % GROUP
    pick = jnp.where(row_code == lane_code, 1.0, 0.0).astype(jnp.bfloat16)
    stacked = jnp.concatenate(
        [queries_ref[:, h * HEAD:(h + 1) * HEAD] for h in range(heads)], axis=0
    )
    placed = jnp.dot(pick, stacked, preferred_element_type=jnp.float32).astype(out_ref.dtype)
    placed = placed.reshape(owners, rows, HEAD)
    for half in range(halves):
        out_ref[:, half] = placed


def fan_kernel(mine_ref, out_ref):
    size = mine_ref.shape[0] // 2
    for target in range(out_ref.shape[0]):
        kv, half = target % 2, target // 2 % 2
        out_ref[target] = mine_ref[half * size:(half + 1) * size, kv * ROWS:(kv + 1) * ROWS]


def attend_kernel(*refs):
    held, query_ref, out_ref = refs[:-2], refs[-2], refs[-1]
    keys = [ref[0] for ref in held]
    wides = [jnp.concatenate([ref[1], jnp.ones_like(ref[1])], axis=1) for ref in held]
    eye = diagonal(HEAD)
    targets, size = out_ref.shape[0], out_ref.shape[1] - 1

    rows = size * ROWS

    def scores_of(target):
        query = query_ref[target * size:(target + 1) * size].reshape(rows, HEAD)
        return [
            lax.dot_general(query, key, (((1,), (1,)), ((), ())), preferred_element_type=jnp.float32)
            for key in keys
        ]

    ahead = scores_of(0)
    for target in range(targets):
        scores = ahead
        if target + 1 < targets:
            ahead = scores_of(target + 1)
        top = jnp.max(functools.reduce(jnp.maximum, scores), axis=1, keepdims=True)
        result = jnp.zeros((rows, 2 * HEAD), jnp.float32)
        for score, wide in zip(scores, wides):
            weights = jnp.exp2((score - top) * (SCALE * LOG2E))
            result = result + jnp.dot(
                weights.astype(jnp.bfloat16), wide, preferred_element_type=jnp.float32
            )
        total = result[:, HEAD:]
        out_ref[target, :size] = (
            (result[:, :HEAD] / total).astype(out_ref.dtype).reshape(size, ROWS, HEAD)
        )
        level = top * SCALE + jnp.log(total)
        levels = jnp.concatenate(
            [to_lanes(level[at:at + HEAD], eye) for at in range(0, rows, HEAD)], axis=0
        )
        pieces = list(pieces_of(levels))
        spare = ROWS - 3 * levels.shape[0]
        if spare:
            pieces.append(jnp.zeros((spare, HEAD), jnp.float32))
        out_ref[target, size] = jnp.concatenate(pieces, axis=0).astype(out_ref.dtype)


def blend_kernel(back_ref, out_ref):
    ring, size = back_ref.shape[0], back_ref.shape[1] - 1
    kvs = (out_ref.shape[1] - STATS) // ROWS
    eye = diagonal(HEAD)
    blocks = HEAD // ROWS
    groups = size // blocks
    lane = iota((HEAD, HEAD), 1)
    table = back_ref[:, size].astype(jnp.float32)
    for half in range(2):
        for group in range(groups):
            here = slice(group * blocks, (group + 1) * blocks)
            there = slice(half * size + group * blocks, half * size + (group + 1) * blocks)
            stats = jnp.zeros((HEAD, HEAD), jnp.float32)
            for kv in range(kvs):
                members = range(kv + 2 * half, ring, CLASSES)
                levels = [
                    table[source, group:group + 1]
                    + table[source, groups + group:groups + group + 1]
                    + table[source, 2 * groups + group:2 * groups + group + 1]
                    for source in members
                ]
                top = functools.reduce(jnp.maximum, levels)
                weights = [jnp.exp(level - top) for level in levels]
                total = sum(weights)
                mixed = jnp.zeros((HEAD, HEAD), jnp.float32)
                for weight, source in zip(weights, members):
                    mean = back_ref[source, here].reshape(HEAD, HEAD).astype(jnp.float32)
                    mixed = mixed + mean * to_column(weight / total, eye)
                out_ref[there, kv * ROWS:(kv + 1) * ROWS] = mixed.astype(out_ref.dtype).reshape(
                    blocks, ROWS, HEAD
                )
                column = to_column(top + jnp.log(total), eye)
                for index, piece in enumerate(pieces_of(column)):
                    stats = jnp.where(lane == kv * 3 + index, piece, stats)
            out_ref[there, kvs * ROWS:] = stats.astype(out_ref.dtype).reshape(blocks, STATS, HEAD)


def tail_kernel(queries_ref, suffix_ref, length_ref, out_ref, max_ref, total_ref):
    requests = queries_ref.shape[0]
    limit = suffix_ref.shape[2]
    length = to_column(
        jnp.broadcast_to(length_ref[...].astype(jnp.float32), (requests, requests)), diagonal(requests)
    ).astype(jnp.int32)
    length = jnp.concatenate([length] * GROUP, axis=0)
    shape = (GROUP * requests, requests * limit)
    row, lane = iota(shape, 0), iota(shape, 1)
    shown = (lane // limit == row % requests) & (lane % limit < length)
    for kv in range(out_ref.shape[0]):
        query = jnp.concatenate(
            [
                queries_ref[:, h * HEAD:(h + 1) * HEAD]
                for h in range(kv * GROUP, (kv + 1) * GROUP)
            ],
            axis=0,
        )
        key = suffix_ref[:, 0, :, kv * HEAD:(kv + 1) * HEAD].reshape(requests * limit, HEAD)
        value = suffix_ref[:, 1, :, kv * HEAD:(kv + 1) * HEAD].reshape(requests * limit, HEAD)
        scores = lax.dot_general(
            query, key, (((1,), (1,)), ((), ())), preferred_element_type=jnp.float32
        ) * SCALE
        scores = jnp.where(shown, scores, -1e30)
        top = jnp.max(scores, axis=1, keepdims=True)
        weights = jnp.where(shown, jnp.exp(scores - top), 0.0)
        total = jnp.sum(weights, axis=1, keepdims=True)
        out_ref[kv] = jnp.dot(weights.astype(jnp.bfloat16), value, preferred_element_type=jnp.float32)
        max_ref[kv] = jnp.broadcast_to(top, max_ref.shape[1:])
        total_ref[kv] = jnp.broadcast_to(total, total_ref.shape[1:])


def merge_kernel(owners_ref, back_ref, tail_ref, max_ref, total_ref, out_ref):
    requests = owners_ref.shape[0]
    owners, halves, kvs = back_ref.shape[0], back_ref.shape[1], tail_ref.shape[0]
    _, slot = slots_of(owners_ref[...])
    slot = jnp.concatenate([slot] * GROUP, axis=0).astype(jnp.int32)
    row = iota((GROUP * requests, 1), 0)
    lane = iota((1, owners * ROWS), 1)
    pick = (slot * GROUP + row // requests) == lane
    pick = jnp.where(pick, 1.0, 0.0).astype(jnp.bfloat16)

    def picked(half, at):
        part = back_ref[:, half, at * ROWS:(at + 1) * ROWS].reshape(owners * ROWS, HEAD)
        return jnp.dot(pick, part, preferred_element_type=jnp.float32)

    stats = [picked(half, kvs) for half in range(halves)]
    for kv in range(kvs):
        levels = [
            stat[:, 3 * kv:3 * kv + 1] + stat[:, 3 * kv + 1:3 * kv + 2] + stat[:, 3 * kv + 2:3 * kv + 3]
            for stat in stats
        ]
        overall = max_ref[kv]
        for level in levels:
            overall = jnp.maximum(overall, level)
        tail_weight = jnp.exp(max_ref[kv] - overall)
        numerator = tail_ref[kv] * tail_weight
        denominator = total_ref[kv] * tail_weight
        for half, level in enumerate(levels):
            weight = jnp.exp(level - overall)
            numerator = numerator + picked(half, kv) * weight
            denominator = denominator + weight
        result = (numerator / denominator).astype(out_ref.dtype)
        for group in range(GROUP):
            head = kv * GROUP + group
            out_ref[:, head * HEAD:(head + 1) * HEAD] = result[group * requests:(group + 1) * requests]


def params():
    return pltpu.CompilerParams(vmem_limit_bytes=VMEM_LIMIT)


def place(owners, queries, owner_count):
    shape = (owner_count, Z_HALVES, SLOTS * queries.shape[1] // HEAD, HEAD)
    return pl.pallas_call(
        place_kernel,
        out_shape=jax.ShapeDtypeStruct(shape, queries.dtype),
        compiler_params=params(),
        name="place",
    )(owners, queries)


def fan(mine, ring):
    shape = (ring, mine.shape[0] // 2, ROWS, HEAD)
    return pl.pallas_call(
        fan_kernel,
        out_shape=jax.ShapeDtypeStruct(shape, mine.dtype),
        compiler_params=params(),
        name="fan",
    )(mine)


def attend(query, held):
    tokens = sum(part.shape[1] for part in held)
    ring, size, rows, width = query.shape
    return pl.pallas_call(
        attend_kernel,
        in_specs=[pl.BlockSpec(memory_space=pltpu.VMEM)] * (len(held) + 1),
        out_specs=pl.BlockSpec(memory_space=pltpu.VMEM),
        out_shape=jax.ShapeDtypeStruct((ring, size + 1, rows, width), query.dtype),
        compiler_params=params(),
        cost_estimate=pl.CostEstimate(
            flops=6 * ring * size * rows * tokens * HEAD,
            bytes_accessed=ring * size * rows * HEAD * 4,
            transcendentals=ring * size * rows * tokens,
        ),
        name="attend",
    )(*held, query.reshape(ring * size, rows, width))


def blend(back, kvs):
    _, size, rows, width = back.shape
    return pl.pallas_call(
        blend_kernel,
        out_shape=jax.ShapeDtypeStruct((2 * (size - 1), kvs * rows + STATS, width), back.dtype),
        compiler_params=params(),
        name="blend",
    )(back)


def tail_attend(queries, suffix_kv, suffix_len):
    kvs = queries.shape[1] // (HEAD * GROUP)
    shape = jax.ShapeDtypeStruct((kvs, GROUP * queries.shape[0], HEAD), jnp.float32)
    return pl.pallas_call(
        tail_kernel,
        out_shape=[shape, shape, shape],
        compiler_params=params(),
        name="tail",
    )(queries, suffix_kv, suffix_len)


def merge(owners, back, tail, top, total, shape, dtype):
    return pl.pallas_call(
        merge_kernel,
        out_shape=jax.ShapeDtypeStruct(shape, dtype),
        compiler_params=params(),
        name="merge",
    )(owners, back, tail, top, total)


def send(array, step):
    ring, cores = lax.axis_size("y"), lax.axis_size("tp")
    pairs = []
    for at in range(ring):
        for core in range(cores):
            to = (at + (step if core == 0 else -step)) % ring
            pairs.append((at * cores + core, to * cores + core))
    return lax.ppermute(array, ("y", "tp"), pairs)


def per_device(queries, prefix_kv, suffix_kv, prefix_map, suffix_len):
    owner_count = lax.axis_size("prefix")
    ring = lax.axis_size("y")
    plane = ("prefix", "zh")
    kvs = queries.shape[1] // (HEAD * GROUP)
    kv = lax.axis_index("y") % 2
    own = lax.dynamic_slice_in_dim(prefix_kv[0], kv * HEAD, HEAD, 2)
    other = lax.dynamic_slice_in_dim(prefix_kv[0], (1 - kv) * HEAD, HEAD, 2)
    far, near = send(own, -2), [send(other, 1), send(other, -1)]
    buckets = place(prefix_map, queries, owner_count)
    buckets = buckets.reshape((owner_count * Z_HALVES,) + buckets.shape[2:])
    mine = lax.all_to_all(buckets, plane, split_axis=0, concat_axis=0, tiled=True)
    mine, far = lax.optimization_barrier((mine, far))
    sent = fan(mine, ring)
    sent, near = lax.optimization_barrier((sent, near))
    query = lax.all_to_all(sent, "y", split_axis=0, concat_axis=0, tiled=True)
    partial = attend(query, [own, far] + near)
    partial, queries = lax.optimization_barrier((partial, queries))
    back = lax.all_to_all(partial, "y", split_axis=0, concat_axis=0, tiled=True)
    tails = tail_attend(queries, suffix_kv, suffix_len)
    blended = blend(back, kvs)
    back = lax.all_to_all(blended, plane, split_axis=0, concat_axis=0, tiled=True)
    back = back.reshape((owner_count, Z_HALVES) + back.shape[1:])
    attended = merge(prefix_map, back, *tails, queries.shape, queries.dtype)
    return lax.all_to_all(attended, "tp", split_axis=0, concat_axis=1, tiled=True)


def solution(mesh):
    prefixes, decs, tps = mesh.devices.shape
    fine = Mesh(
        mesh.devices.reshape(prefixes, Z_HALVES, decs // Z_HALVES, tps), ("prefix", "zh", "y", "tp")
    )
    owner = ("prefix", "zh", "y")
    return jax.shard_map(
        per_device,
        mesh=fine,
        in_specs=(
            P(owner, "tp"),
            P("prefix", None, ("zh", "y"), "tp"),
            P(owner, None, None, "tp"),
            P(owner, None),
            P(owner, None),
        ),
        out_specs=P(owner + ("tp",), None),
        check_vma=False,
    )
```

```python
import functools
import math

import jax
import jax.numpy as jnp
from jax import lax
from jax.experimental import pallas as pl
from jax.experimental.pallas import tpu as pltpu
from jax.sharding import Mesh, PartitionSpec as P

HEAD = 128
GROUP = 8
SLOTS = 2
ROWS = SLOTS * GROUP
SCALE = HEAD ** (-0.5)
LOG2E = math.log2(math.e)
STATS = 8
Z_HALVES = 2
CLASSES = 4
VMEM_LIMIT = 48 * 1024 * 1024


def iota(shape, dim):
    return lax.broadcasted_iota(jnp.int32, shape, dim)


def diagonal(size):
    return iota((size, size), 0) == iota((size, size), 1)


def to_lanes(column, eye):
    return jnp.sum(jnp.where(eye, column, 0.0), axis=0, keepdims=True)


def to_column(lanes, eye):
    return jnp.sum(jnp.where(eye, lanes, 0.0), axis=1, keepdims=True)


def slots_of(owners):
    count = owners.shape[0]
    owner_column = owners.astype(jnp.float32)
    owner_lanes = to_lanes(owner_column, diagonal(count))
    same = owner_column == owner_lanes
    row, lane = iota((count, count), 0), iota((count, count), 1)
    rank_lanes = jnp.sum(jnp.where(same & (row < lane), 1.0, 0.0), axis=0, keepdims=True)
    rank_column = jnp.sum(jnp.where(same & (lane < row), 1.0, 0.0), axis=1, keepdims=True)
    return owner_lanes * SLOTS + rank_lanes, owner_column * SLOTS + rank_column


def pieces_of(value):
    first = value.astype(jnp.bfloat16).astype(jnp.float32)
    second = (value - first).astype(jnp.bfloat16).astype(jnp.float32)
    return first, second, value - first - second


def place_kernel(owners_ref, queries_ref, out_ref):
    requests, heads = queries_ref.shape[0], queries_ref.shape[1] // HEAD
    slot_lanes, _ = slots_of(owners_ref[...])
    width = heads * requests
    spread = jnp.where(iota((requests, width), 1) % requests == iota((requests, width), 0), 1.0, 0.0)
    slot_wide = jnp.dot(
        jnp.broadcast_to(slot_lanes, (8, requests)).astype(jnp.bfloat16),
        spread.astype(jnp.bfloat16),
        preferred_element_type=jnp.float32,
    )[0:1]
    lane_code = slot_wide.astype(jnp.int32) * heads + iota((1, width), 1) // requests
    owners, halves, rows = out_ref.shape[:3]
    row = iota((owners * rows, 1), 0)
    slot = (row // rows) * SLOTS + (row // GROUP) % SLOTS
    row_code = slot * heads + (row // ROWS) % (heads // GROUP) * GROUP + row % GROUP
    pick = jnp.where(row_code == lane_code, 1.0, 0.0).astype(jnp.bfloat16)
    stacked = jnp.concatenate(
        [queries_ref[:, h * HEAD:(h + 1) * HEAD] for h in range(heads)], axis=0
    )
    placed = jnp.dot(pick, stacked, preferred_element_type=jnp.float32).astype(out_ref.dtype)
    placed = placed.reshape(owners, rows, HEAD)
    for half in range(halves):
        out_ref[:, half] = placed


def fan_kernel(mine_ref, out_ref):
    size = mine_ref.shape[0] // 2
    for target in range(out_ref.shape[0]):
        kv, half = target % 2, target // 2 % 2
        out_ref[target] = mine_ref[half * size:(half + 1) * size, kv * ROWS:(kv + 1) * ROWS]


def attend_kernel(*refs):
    held, query_ref, out_ref = refs[:-2], refs[-2], refs[-1]
    keys = [ref[0] for ref in held]
    wides = [jnp.concatenate([ref[1], jnp.ones_like(ref[1])], axis=1) for ref in held]
    eye = diagonal(HEAD)
    targets, size = out_ref.shape[0], out_ref.shape[1] - 1

    rows = size * ROWS

    def scores_of(target):
        query = query_ref[target * size:(target + 1) * size].reshape(rows, HEAD)
        return [
            lax.dot_general(query, key, (((1,), (1,)), ((), ())), preferred_element_type=jnp.float32)
            for key in keys
        ]

    ahead = scores_of(0)
    for target in range(targets):
        scores = ahead
        if target + 1 < targets:
            ahead = scores_of(target + 1)
        top = jnp.max(functools.reduce(jnp.maximum, scores), axis=1, keepdims=True)
        result = jnp.zeros((rows, 2 * HEAD), jnp.float32)
        for score, wide in zip(scores, wides):
            weights = jnp.exp2((score - top) * (SCALE * LOG2E))
            result = result + jnp.dot(
                weights.astype(jnp.bfloat16), wide, preferred_element_type=jnp.float32
            )
        total = result[:, HEAD:]
        out_ref[target, :size] = (
            (result[:, :HEAD] / total).astype(out_ref.dtype).reshape(size, ROWS, HEAD)
        )
        level = top * SCALE + jnp.log(total)
        levels = jnp.concatenate(
            [to_lanes(level[at:at + HEAD], eye) for at in range(0, rows, HEAD)], axis=0
        )
        pieces = list(pieces_of(levels))
        spare = ROWS - 3 * levels.shape[0]
        if spare:
            pieces.append(jnp.zeros((spare, HEAD), jnp.float32))
        out_ref[target, size] = jnp.concatenate(pieces, axis=0).astype(out_ref.dtype)


def blend_kernel(back_ref, out_ref):
    ring, size = back_ref.shape[0], back_ref.shape[1] - 1
    kvs = (out_ref.shape[1] - STATS) // ROWS
    eye = diagonal(HEAD)
    blocks = HEAD // ROWS
    groups = size // blocks
    table = back_ref[:, size].astype(jnp.float32)
    for half in range(2):
        for group in range(groups):
            here = slice(group * blocks, (group + 1) * blocks)
            there = slice(half * size + group * blocks, half * size + (group + 1) * blocks)
            stats = []
            for kv in range(kvs):
                members = range(kv + 2 * half, ring, CLASSES)
                levels = [
                    table[source, group:group + 1]
                    + table[source, groups + group:groups + group + 1]
                    + table[source, 2 * groups + group:2 * groups + group + 1]
                    for source in members
                ]
                top = functools.reduce(jnp.maximum, levels)
                weights = [jnp.exp(level - top) for level in levels]
                total = sum(weights)
                mixed = jnp.zeros((HEAD, HEAD), jnp.float32)
                for weight, source in zip(weights, members):
                    mean = back_ref[source, here].reshape(HEAD, HEAD).astype(jnp.float32)
                    mixed = mixed + mean * to_column(weight / total, eye)
                out_ref[there, kv * ROWS:(kv + 1) * ROWS] = mixed.astype(out_ref.dtype).reshape(
                    blocks, ROWS, HEAD
                )
                stats += pieces_of(top + jnp.log(total))
            stats.append(jnp.zeros((STATS - len(stats), HEAD), jnp.float32))
            stats = jnp.concatenate(stats, axis=0).astype(out_ref.dtype)
            out_ref[there, kvs * ROWS:] = jnp.broadcast_to(stats[None], (blocks, STATS, HEAD))


def tail_kernel(queries_ref, suffix_ref, length_ref, out_ref, max_ref, total_ref):
    requests = queries_ref.shape[0]
    limit = suffix_ref.shape[2]
    length = to_column(
        jnp.broadcast_to(length_ref[...].astype(jnp.float32), (requests, requests)), diagonal(requests)
    ).astype(jnp.int32)
    length = jnp.concatenate([length] * GROUP, axis=0)
    shape = (GROUP * requests, requests * limit)
    row, lane = iota(shape, 0), iota(shape, 1)
    shown = (lane // limit == row % requests) & (lane % limit < length)
    for kv in range(out_ref.shape[0]):
        query = jnp.concatenate(
            [
                queries_ref[:, h * HEAD:(h + 1) * HEAD]
                for h in range(kv * GROUP, (kv + 1) * GROUP)
            ],
            axis=0,
        )
        key = suffix_ref[:, 0, :, kv * HEAD:(kv + 1) * HEAD].reshape(requests * limit, HEAD)
        value = suffix_ref[:, 1, :, kv * HEAD:(kv + 1) * HEAD].reshape(requests * limit, HEAD)
        scores = lax.dot_general(
            query, key, (((1,), (1,)), ((), ())), preferred_element_type=jnp.float32
        ) * SCALE
        scores = jnp.where(shown, scores, -1e30)
        top = jnp.max(scores, axis=1, keepdims=True)
        weights = jnp.where(shown, jnp.exp(scores - top), 0.0)
        total = jnp.sum(weights, axis=1, keepdims=True)
        out_ref[kv] = jnp.dot(weights.astype(jnp.bfloat16), value, preferred_element_type=jnp.float32)
        max_ref[kv] = jnp.broadcast_to(top, max_ref.shape[1:])
        total_ref[kv] = jnp.broadcast_to(total, total_ref.shape[1:])


def merge_kernel(spot_ref, owners_ref, back_ref, tail_ref, max_ref, total_ref, out_ref):
    requests = owners_ref.shape[0]
    owners, halves, kvs = back_ref.shape[0], back_ref.shape[1], tail_ref.shape[0]
    _, slot = slots_of(owners_ref[...])
    slot = jnp.concatenate([slot] * GROUP, axis=0).astype(jnp.int32)
    row = iota((GROUP * requests, 1), 0)
    lane = iota((1, owners * ROWS), 1)
    place_of = slot * GROUP + row // requests
    pick = jnp.where(place_of == lane, 1.0, 0.0).astype(jnp.bfloat16)
    stat_lane = iota((1, owners * STATS), 1)
    owned = stat_lane // STATS == slot // SLOTS
    wanted = iota((1, HEAD), 1) == spot_ref[0, 0] * ROWS + place_of % ROWS

    def picked(half, at):
        part = back_ref[:, half, at * ROWS:(at + 1) * ROWS].reshape(owners * ROWS, HEAD)
        return jnp.dot(pick, part, preferred_element_type=jnp.float32)

    def level_of(half, kv):
        table = back_ref[:, half, kvs * ROWS:].astype(jnp.float32).reshape(owners * STATS, HEAD)
        mine = owned & (stat_lane % STATS // 3 == kv)
        level = jnp.dot(
            jnp.where(mine, 1.0, 0.0).astype(jnp.bfloat16),
            table.astype(jnp.bfloat16),
            preferred_element_type=jnp.float32,
        )
        return jnp.sum(jnp.where(wanted, level, 0.0), axis=1, keepdims=True)

    for kv in range(kvs):
        levels = [level_of(half, kv) for half in range(halves)]
        overall = max_ref[kv]
        for level in levels:
            overall = jnp.maximum(overall, level)
        tail_weight = jnp.exp(max_ref[kv] - overall)
        numerator = tail_ref[kv] * tail_weight
        denominator = total_ref[kv] * tail_weight
        for half, level in enumerate(levels):
            weight = jnp.exp(level - overall)
            numerator = numerator + picked(half, kv) * weight
            denominator = denominator + weight
        result = (numerator / denominator).astype(out_ref.dtype)
        for group in range(GROUP):
            head = kv * GROUP + group
            out_ref[:, head * HEAD:(head + 1) * HEAD] = result[group * requests:(group + 1) * requests]


def params():
    return pltpu.CompilerParams(vmem_limit_bytes=VMEM_LIMIT)


def place(owners, queries, owner_count):
    shape = (owner_count, Z_HALVES, SLOTS * queries.shape[1] // HEAD, HEAD)
    return pl.pallas_call(
        place_kernel,
        out_shape=jax.ShapeDtypeStruct(shape, queries.dtype),
        compiler_params=params(),
        name="place",
    )(owners, queries)


def fan(mine, ring):
    shape = (ring, mine.shape[0] // 2, ROWS, HEAD)
    return pl.pallas_call(
        fan_kernel,
        out_shape=jax.ShapeDtypeStruct(shape, mine.dtype),
        compiler_params=params(),
        name="fan",
    )(mine)


def attend(query, held):
    tokens = sum(part.shape[1] for part in held)
    ring, size, rows, width = query.shape
    return pl.pallas_call(
        attend_kernel,
        in_specs=[pl.BlockSpec(memory_space=pltpu.VMEM)] * (len(held) + 1),
        out_specs=pl.BlockSpec(memory_space=pltpu.VMEM),
        out_shape=jax.ShapeDtypeStruct((ring, size + 1, rows, width), query.dtype),
        compiler_params=params(),
        cost_estimate=pl.CostEstimate(
            flops=6 * ring * size * rows * tokens * HEAD,
            bytes_accessed=ring * size * rows * HEAD * 4,
            transcendentals=ring * size * rows * tokens,
        ),
        name="attend",
    )(*held, query.reshape(ring * size, rows, width))


def blend(back, kvs):
    _, size, rows, width = back.shape
    return pl.pallas_call(
        blend_kernel,
        out_shape=jax.ShapeDtypeStruct((2 * (size - 1), kvs * rows + STATS, width), back.dtype),
        compiler_params=params(),
        name="blend",
    )(back)


def tail_attend(queries, suffix_kv, suffix_len):
    kvs = queries.shape[1] // (HEAD * GROUP)
    shape = jax.ShapeDtypeStruct((kvs, GROUP * queries.shape[0], HEAD), jnp.float32)
    return pl.pallas_call(
        tail_kernel,
        out_shape=[shape, shape, shape],
        compiler_params=params(),
        name="tail",
    )(queries, suffix_kv, suffix_len)


def merge(spot, owners, back, tail, top, total, shape, dtype):
    vmem = pl.BlockSpec(memory_space=pltpu.VMEM)
    return pl.pallas_call(
        merge_kernel,
        in_specs=[pl.BlockSpec(memory_space=pltpu.SMEM)] + [vmem] * 5,
        out_specs=vmem,
        out_shape=jax.ShapeDtypeStruct(shape, dtype),
        compiler_params=params(),
        name="merge",
    )(spot, owners, back, tail, top, total)


def send(array, step):
    ring, cores = lax.axis_size("y"), lax.axis_size("tp")
    pairs = []
    for at in range(ring):
        for core in range(cores):
            to = (at + (step if core == 0 else -step)) % ring
            pairs.append((at * cores + core, to * cores + core))
    return lax.ppermute(array, ("y", "tp"), pairs)


def per_device(queries, prefix_kv, suffix_kv, prefix_map, suffix_len):
    owner_count = lax.axis_size("prefix")
    ring = lax.axis_size("y")
    plane = ("prefix", "zh")
    kvs = queries.shape[1] // (HEAD * GROUP)
    kv = lax.axis_index("y") % 2
    own = lax.dynamic_slice_in_dim(prefix_kv[0], kv * HEAD, HEAD, 2)
    other = lax.dynamic_slice_in_dim(prefix_kv[0], (1 - kv) * HEAD, HEAD, 2)
    far, near = send(own, -2), [send(other, 1), send(other, -1)]
    buckets = place(prefix_map, queries, owner_count)
    buckets = buckets.reshape((owner_count * Z_HALVES,) + buckets.shape[2:])
    mine = lax.all_to_all(buckets, plane, split_axis=0, concat_axis=0, tiled=True)
    mine, far = lax.optimization_barrier((mine, far))
    sent = fan(mine, ring)
    sent, near = lax.optimization_barrier((sent, near))
    query = lax.all_to_all(sent, "y", split_axis=0, concat_axis=0, tiled=True)
    partial = attend(query, [own, far] + near)
    partial, queries = lax.optimization_barrier((partial, queries))
    back = lax.all_to_all(partial, "y", split_axis=0, concat_axis=0, tiled=True)
    tails = tail_attend(queries, suffix_kv, suffix_len)
    blended = blend(back, kvs)
    back = lax.all_to_all(blended, plane, split_axis=0, concat_axis=0, tiled=True)
    back = back.reshape((owner_count, Z_HALVES) + back.shape[1:])
    spot = (lax.axis_index(plane) % (HEAD // ROWS)).astype(jnp.int32).reshape(1, 1)
    attended = merge(spot, prefix_map, back, *tails, queries.shape, queries.dtype)
    return lax.all_to_all(attended, "tp", split_axis=0, concat_axis=1, tiled=True)


def solution(mesh):
    prefixes, decs, tps = mesh.devices.shape
    fine = Mesh(
        mesh.devices.reshape(prefixes, Z_HALVES, decs // Z_HALVES, tps), ("prefix", "zh", "y", "tp")
    )
    owner = ("prefix", "zh", "y")
    return jax.shard_map(
        per_device,
        mesh=fine,
        in_specs=(
            P(owner, "tp"),
            P("prefix", None, ("zh", "y"), "tp"),
            P(owner, None, None, "tp"),
            P(owner, None),
            P(owner, None),
        ),
        out_specs=P(owner + ("tp",), None),
        check_vma=False,
    )
```
